256 devices in a mesh: seq: 64 (over y, z, core), tp: 4 (over x).
Axes of the slice: x: 4, y: 4, z: 8, core: 2. Of those that a mesh axis runs over, the one named last changes fastest.
Arguments:
- query_in: bfloat16 [16384, 2048], P('seq', 'tp'), may hold values from -6 to 6
- key_in: bfloat16 [16384, 2048], P('seq', 'tp'), may hold values from -6 to 6
- value_in: bfloat16 [16384, 2048], P('seq', 'tp'), may hold values from -6 to 6
- short_filter: float32 [3, 3, 2048], P(None, None, 'tp'), may hold values from -3 to 3
- skip_gain: float32 [2048], P('tp'), may hold values from 0.5 to 1.5
- filter_taps: float32 [16384, 2048], P('seq', 'tp'), may hold values from -1.2 to 1.2
- out_weight: bfloat16 [2048, 4096], P('tp'), may hold values from -0.125 to 0.125
- out_grad: bfloat16 [16384, 4096], P(('seq', 'tp')), may hold values from -6 to 6
Outputs:
- mixed_out: bfloat16 [16384, 4096], P(('seq', 'tp'))
- grad_query: bfloat16 [16384, 2048], P('seq', 'tp')
- grad_key: bfloat16 [16384, 2048], P('seq', 'tp')
- grad_value: bfloat16 [16384, 2048], P('seq', 'tp')
- filter_grad: float32 [16384, 2048], P('seq', 'tp')
The draws below stay inside these ranges and needn't reach their ends.
All inputs are finite; a program needn't handle non-finite values.
Results may differ from the reference program's by a relative error of at most 0.015.
Values may be sent and summed in bfloat16 or wider, within the bound.
A program may use at most 128 MiB of HBM per device.

```python
import math
import jax
import jax.numpy as jnp
from jax import lax

D = 4096
C = 2048
SEQ = 16384


def shared_stream(key):
    return jax.random.truncated_normal(key, -6.0, 6.0, (SEQ, C))


def draw_key_in(key, part):
    shared = shared_stream(key)
    return shared.astype(jnp.bfloat16)


def draw_value_in(key, part):
    shared = shared_stream(key)
    key = jax.random.fold_in(key, 13)
    own_part = jax.random.truncated_normal(key, -6.0, 6.0, (SEQ, C))
    return jnp.clip(0.6 * shared + 0.8 * own_part, -6.0, 6.0).astype(jnp.bfloat16)


def draw_filter_taps(key, part):
    key = jax.random.fold_in(key, 7)
    pick_key, slow_key, fast_key, rough_key, floor_key, sign_key, level_key = jax.random.split(key, 7)
    fast_share = 0.5
    fast_mask = jax.random.uniform(pick_key, (C,)) < fast_share
    slow_rate = jax.random.uniform(slow_key, (C,), minval=0.2, maxval=2.0) / SEQ
    fast_rate = 1.0 / jax.random.uniform(fast_key, (C,), minval=30.0, maxval=160.0)
    decay_rate = jnp.where(fast_mask, fast_rate, slow_rate)
    amplitude = jnp.sqrt(jnp.expm1(-2.0 * decay_rate) / jnp.expm1(-2.0 * decay_rate * SEQ))
    lag_pos = jnp.arange(SEQ, dtype=jnp.float32)[:, None]
    rough_noise = jax.random.truncated_normal(rough_key, -4.0, 4.0, (SEQ, C))
    floor_rough = 0.002 * jax.random.uniform(floor_key, (SEQ, C), minval=-1.0, maxval=1.0)
    floor_sign = jnp.where(jax.random.uniform(sign_key, (C,)) < 0.5, -1.0, 1.0)
    floor_level = floor_sign * 0.0001 * jax.random.uniform(level_key, (C,), minval=0.5, maxval=1.5)
    head = amplitude * jnp.exp(-decay_rate * lag_pos) * rough_noise
    return (head + floor_rough + floor_level).astype(jnp.float32)


def level_of(rng, dims, shards, smallest, largest):
    factor_of, own = 1.0, jax.random.fold_in(rng, 6)
    for position, parts in shards:
        heights = jnp.exp(jax.random.uniform(jax.random.fold_in(own, position), (parts,), jnp.float32, smallest / len(shards), largest / len(shards)))
        factor_of = factor_of * jnp.repeat(heights, dims[position] // parts).reshape([-1 if axis == position else 1 for axis in range(len(dims))])
    return factor_of


def bell_draw(key, shape, deviation, bound, pieces=(), kind=jnp.bfloat16):
    entries = deviation * jax.random.normal(key, shape, jnp.float32)
    if pieces:
        entries = entries * level_of(key, shape, pieces, -0.22, 0.18)
    return jnp.clip(entries, -bound, bound).astype(kind)


def setup_inputs(seed: int = 0) -> dict:
    keys = jax.random.split(jax.random.key(seed), 9)
    return {
        "query_in": bell_draw(keys[0], (SEQ, C), 1.0, 6.0, ((0, 64), (1, 4))),
        "key_in": draw_key_in(jax.random.fold_in(keys[8], 71), 0),
        "value_in": draw_value_in(jax.random.fold_in(keys[8], 71), 0),
        "short_filter": bell_draw(keys[3], (3, 3, C), 0.6, 3.0, ((2, 4),), jnp.float32),
        "skip_gain": jnp.clip(0.5 + 1.0 * jax.random.uniform(keys[4], (C,), jnp.float32) ** level_of(keys[4], (C,), ((0, 4),), -0.2, 0.2), 0.5, 1.5),
        "filter_taps": draw_filter_taps(jax.random.fold_in(keys[8], 71), 0),
        "out_weight": bell_draw(keys[6], (C, D), C ** -0.5, 0.125, ((0, 4),)),
        "out_grad": bell_draw(keys[7], (SEQ, D), 1.0, 6.0, ((0, 256),)),
    }


def causal_block(taps_blk, sig_blk):
    full_len = 2 * SEQ
    taps_spec = jnp.fft.rfft(taps_blk, n=full_len, axis=0)
    sig_spec = jnp.fft.rfft(sig_blk, n=full_len, axis=0)
    return (jnp.fft.irfft(taps_spec * sig_spec, n=full_len, axis=0)[:SEQ],)

def adjoint_block(taps_blk, sig_blk, grad_blk):
    full_len = 2 * SEQ
    taps_spec = jnp.fft.rfft(taps_blk, n=full_len, axis=0)
    sig_spec = jnp.fft.rfft(sig_blk, n=full_len, axis=0)
    grad_spec = jnp.fft.rfft(grad_blk, n=full_len, axis=0)
    first_out = jnp.fft.irfft(jnp.conj(taps_spec) * grad_spec, n=full_len, axis=0)[:SEQ]
    second_out = jnp.fft.irfft(jnp.conj(sig_spec) * grad_spec, n=full_len, axis=0)[:SEQ]
    return (first_out, second_out)

def by_blocks(block_fn, arrays):
    chan_block = math.gcd(C, 128)
    block_count = C // chan_block
    folded = tuple((array_in.reshape(SEQ, block_count, chan_block).transpose(1, 0, 2) for array_in in arrays))

    def apply_group(group):
        return block_fn(*group)
    results = lax.map(apply_group, folded)
    return tuple((result_blk.transpose(1, 0, 2).reshape(SEQ, C) for result_blk in results))

def reference(query_in, key_in, value_in, short_filter, skip_gain, filter_taps, out_weight, out_grad):
    streams = jnp.stack([query_in, key_in, value_in]).astype(jnp.float32)
    padded = jnp.pad(streams, ((0, 0), (2, 0), (0, 0)))
    shortened = (short_filter[:, 0:1, :] * padded[:, 2:, :] + short_filter[:, 1:2, :] * padded[:, 1:-1, :] + short_filter[:, 2:3, :] * padded[:, :-2, :]).astype(jnp.bfloat16)
    q_short = shortened[0].astype(jnp.float32)
    k_short = shortened[1].astype(jnp.float32)
    v_short = shortened[2].astype(jnp.float32)
    signal = k_short * v_short
    conv_part, = by_blocks(causal_block, (filter_taps, signal))
    response = skip_gain * signal + conv_part
    gate_out = (q_short * response).astype(jnp.bfloat16)
    mixed_out = jnp.dot(gate_out, out_weight, preferred_element_type=jnp.float32).astype(jnp.bfloat16)
    grad_gate = lax.dot_general(out_grad, out_weight, (((1,), (1,)), ((), ())), preferred_element_type=jnp.float32)
    grad_q_short = grad_gate * response
    grad_resp = grad_gate * q_short
    adj_part, corr_part = by_blocks(adjoint_block, (filter_taps, signal, grad_resp))
    grad_signal = skip_gain * grad_resp + adj_part
    filter_grad = corr_part * (1.0 / math.sqrt(SEQ))
    grad_stack = jnp.stack([grad_q_short, grad_signal * v_short, grad_signal * k_short])
    grad_ext = jnp.pad(grad_stack, ((0, 0), (0, 2), (0, 0)))
    stream_grads = (short_filter[:, 0:1, :] * grad_ext[:, :-2, :] + short_filter[:, 1:2, :] * grad_ext[:, 1:-1, :] + short_filter[:, 2:3, :] * grad_ext[:, 2:, :]).astype(jnp.bfloat16)
    return (mixed_out, stream_grads[0], stream_grads[1], stream_grads[2], filter_grad)
```

```python
import functools
import math

import jax
import jax.numpy as jnp
import numpy as np
from jax import lax
from jax.experimental import pallas as pl
from jax.experimental.pallas import tpu as pltpu
from jax.sharding import PartitionSpec as P

MESH = pl.DeviceIdType.MESH
BF16, F32 = jnp.bfloat16, jnp.float32
LANES = 128


def tables(shards, rows):
    outer, full = 2 * shards, 2 * shards * rows
    half = outer // 2 + 1
    padded = -(-half // 8) * 8
    freq, shard, row = np.arange(half), np.arange(shards), np.arange(rows)
    outer_angle = 2 * np.pi * (freq[:, None] * shard[None] % outer) / outer
    twist_angle = 2 * np.pi * (freq[:, None] * row[None] % full) / full
    inner_angle = 2 * np.pi * (row[:, None] * row[None] % rows) / rows
    first = np.zeros((2 * padded, shards))
    first[:half], first[padded : padded + half] = np.cos(outer_angle), -np.sin(outer_angle)
    twist = np.zeros((2, padded, rows))
    twist[0, :half], twist[1, :half] = np.cos(twist_angle), -np.sin(twist_angle)
    cos, sin = np.cos(inner_angle), -np.sin(inner_angle)
    inner = np.block([[cos, sin], [-sin, cos]])
    weight = np.full((half, 1), 2.0 / full)
    weight[0] = weight[-1] = 1.0 / full
    last = np.zeros((shards, 2 * padded))
    last[:, :half] = (weight * np.cos(outer_angle)).T
    last[:, padded : padded + half] = -(weight * np.sin(outer_angle)).T
    as_bf16 = lambda a: jnp.asarray(a.astype(np.float32)).astype(BF16)
    return (
        as_bf16(first),
        jnp.asarray(twist.astype(np.float32)),
        as_bf16(inner),
        as_bf16(inner.T),
        as_bf16(last),
    )


def dot(a, b):
    return jnp.dot(a, b, preferred_element_type=F32)


def enter(n):
    me = lax.axis_index("seq")
    barrier = pltpu.get_barrier_semaphore()

    def greet(i, carry):
        pl.semaphore_signal(
            barrier, inc=1, device_id={"seq": lax.rem(me + i, n)}, device_id_type=MESH
        )
        return carry

    lax.fori_loop(1, n, greet, 0)
    pl.semaphore_wait(barrier, n - 1)
    return me


def exchange_start(me, n, send, recv, sems):
    def push(i, carry):
        peer = lax.rem(me + i, n)
        pltpu.make_async_remote_copy(
            src_ref=send.at[peer],
            dst_ref=recv.at[me],
            send_sem=sems.at[0],
            recv_sem=sems.at[1],
            device_id={"seq": peer},
            device_id_type=MESH,
        ).start()
        return carry

    lax.fori_loop(1, n, push, 0)
    recv[pl.ds(me, 1)] = send[pl.ds(me, 1)]


def whole(me, n, send, recv, sems):
    return pltpu.make_async_remote_copy(
        src_ref=send.at[pl.ds(0, n - 1)],
        dst_ref=recv.at[pl.ds(0, n - 1)],
        send_sem=sems.at[0],
        recv_sem=sems.at[1],
        device_id={"seq": lax.rem(me + 1, n)},
        device_id_type=MESH,
    )


def pack(value, send, n):
    halves = [
        value[h * LANES : (h + 1) * LANES].T.reshape(n, 8, LANES) for h in range(2)
    ]
    send[...] = jnp.concatenate(halves, axis=1).astype(BF16)


def unpack(recv, n):
    value = recv[...].astype(F32)
    return jnp.concatenate(
        [value[:, 8 * h : 8 * h + 8].reshape(8 * n, LANES).T for h in range(2)], axis=0
    )


def spectrum(n, recv, tabs, rowed, mid, out):
    first, twist, inner = tabs[:3]
    padded = twist.shape[1]
    width = twist.shape[2]
    rowed[...] = recv[...].astype(F32).reshape(16 * n, LANES)
    for c in range(8):
        x = jnp.concatenate(
            [rowed[pl.ds(8 * h + c, n, stride=16), :] for h in range(2)], axis=1
        ).astype(BF16)
        a = dot(first[...], x)
        re, im = a[:padded], a[padded:]
        rows = pl.ds(c * padded, padded)
        mid[rows, :width] = re * twist[0] - im * twist[1]
        mid[rows, width:] = re * twist[1] + im * twist[0]
    out[...] = dot(mid[...].astype(BF16), inner[...])


def synthesis(n, tabs, rowed, mid, send):
    twist, back, last = tabs[1], tabs[3], tabs[4]
    padded = twist.shape[1]
    width = twist.shape[2]
    mid[...] = dot(mid[...].astype(BF16), back[...])
    for c in range(8):
        rows = pl.ds(c * padded, padded)
        re, im = mid[rows, :width], mid[rows, width:]
        turned = jnp.concatenate(
            [re * twist[0] + im * twist[1], im * twist[0] - re * twist[1]], axis=0
        ).astype(BF16)
        y = dot(last[...], turned)
        for h in range(2):
            rowed[pl.ds(8 * h + c, n, stride=16), :] = y[:, h * LANES : (h + 1) * LANES]
    send[...] = rowed[...].reshape(n, 16, LANES).astype(BF16)


def front(
    n, query, key, value, taps, short, gain, first, twist, inner, back, last,
    q_out, k_out, v_out, response_out, gate_out, sig_spec, tap_spec,
    ext, halo, rowed, mid, send, recv, halo_sems, sems,
):
    tabs = (first, twist, inner, back, last)
    tokens = query.shape[0]
    me = enter(n)
    streams = (query, key, value)
    edges = []
    for s, stream in enumerate(streams):
        edge = pltpu.make_async_remote_copy(
            src_ref=stream.at[pl.ds(tokens - 16, 16)],
            dst_ref=halo.at[s],
            send_sem=halo_sems.at[0, s],
            recv_sem=halo_sems.at[1, s],
            device_id={"seq": lax.rem(me + 1, n)},
            device_id_type=MESH,
        )
        edge.start()
        edges.append(edge)
    pack(taps[...], send.at[0], n)
    exchange_start(me, n, send.at[0], recv.at[0], sems.at[0])
    shortened = [None] * 3
    for s in (1, 2, 0):
        ext[s, pl.ds(8, tokens)] = streams[s][...].astype(F32)
        edges[s].wait_recv()
        edge_rows = halo[s].astype(F32)[8:]
        ext[s, pl.ds(0, 8)] = jnp.where(me > 0, edge_rows, 0.0)
        shortened[s] = (
            short[s, 0:1, :] * ext[s, pl.ds(8, tokens)]
            + short[s, 1:2, :] * ext[s, pl.ds(7, tokens)]
            + short[s, 2:3, :] * ext[s, pl.ds(6, tokens)]
        ).astype(BF16)
        if s == 2:
            k_out[...] = shortened[1]
            v_out[...] = shortened[2]
            signal = shortened[1].astype(F32) * shortened[2].astype(F32)
            pack(signal, send.at[1], n)
            exchange_start(me, n, send.at[1], recv.at[1], sems.at[1])
            response_out[...] = gain[...] * signal
    q_out[...] = shortened[0]
    whole(me, n, send.at[0], recv.at[0], sems.at[0]).wait_recv()
    spectrum(n, recv.at[0], tabs, rowed, mid, tap_spec)
    whole(me, n, send.at[1], recv.at[1], sems.at[1]).wait_recv()
    spectrum(n, recv.at[1], tabs, rowed, mid, sig_spec)
    width = twist.shape[2]
    ar, ai = tap_spec[:, :width], tap_spec[:, width:]
    br, bi = sig_spec[:, :width], sig_spec[:, width:]
    mid[:, :width] = ar * br - ai * bi
    mid[:, width:] = ar * bi + ai * br
    synthesis(n, tabs, rowed, mid, send.at[2])
    exchange_start(me, n, send.at[2], recv.at[2], sems.at[2])
    whole(me, n, send.at[2], recv.at[2], sems.at[2]).wait_recv()
    response = response_out[...] + unpack(recv.at[2], n)
    response_out[...] = response
    gate_out[...] = (q_out[...].astype(F32) * response).astype(BF16)
    for edge in edges:
        edge.wait_send()
    for i in range(3):
        whole(me, n, send.at[i], recv.at[i], sems.at[i]).wait_send()


def project(gate, weight, grad, mixed, grad_gate):
    part = lax.dot_general(
        grad[...], weight[...], (((1,), (1,)), ((), ())), preferred_element_type=F32
    )

    @pl.when(pl.program_id(0) == 0)
    def _():
        grad_gate[...] = part

    @pl.when(pl.program_id(0) > 0)
    def _():
        grad_gate[...] += part

    mixed[...] = dot(gate[...], weight[...]).astype(BF16)


def rear(
    n, q_short, k_short, v_short, response, grad_gate, short, gain, sig_spec, tap_spec,
    first, twist, inner, back, last,
    query_out, key_out, value_out, taps_out,
    ext, spec, rowed, mid, send, recv, halo_sems, sems,
):
    tabs = (first, twist, inner, back, last)
    tokens = q_short.shape[0]
    width = twist.shape[2]
    me = enter(n)
    grad_response = grad_gate[...] * q_short[...].astype(F32)
    pack(grad_response, send.at[0], n)
    exchange_start(me, n, send.at[0], recv.at[0], sems.at[0])
    ext[0, pl.ds(0, tokens)] = grad_gate[...] * response[...]
    whole(me, n, send.at[0], recv.at[0], sems.at[0]).wait_recv()
    spectrum(n, recv.at[0], tabs, rowed, mid, spec)
    for i, other in ((1, tap_spec), (2, sig_spec)):
        ar, ai = other[:, :width], other[:, width:]
        br, bi = spec[:, :width], spec[:, width:]
        mid[:, :width] = ar * br + ai * bi
        mid[:, width:] = ar * bi - ai * br
        synthesis(n, tabs, rowed, mid, send.at[i])
        exchange_start(me, n, send.at[i], recv.at[i], sems.at[i])
    whole(me, n, send.at[1], recv.at[1], sems.at[1]).wait_recv()
    grad_signal = gain[...] * (grad_gate[...] * q_short[...].astype(F32)) + unpack(
        recv.at[1], n
    )
    ext[1, pl.ds(0, tokens)] = grad_signal * v_short[...].astype(F32)
    ext[2, pl.ds(0, tokens)] = grad_signal * k_short[...].astype(F32)
    edges = []
    for s in range(3):
        edge = pltpu.make_async_remote_copy(
            src_ref=ext.at[s, pl.ds(0, 8)],
            dst_ref=ext.at[s, pl.ds(tokens, 8)],
            send_sem=halo_sems.at[0, s],
            recv_sem=halo_sems.at[1, s],
            device_id={"seq": lax.rem(me + n - 1, n)},
            device_id_type=MESH,
        )
        edge.start()
        edges.append(edge)
    whole(me, n, send.at[2], recv.at[2], sems.at[2]).wait_recv()
    taps_out[...] = unpack(recv.at[2], n) * (1.0 / math.sqrt(tokens * n))
    for s, out in enumerate((query_out, key_out, value_out)):
        edges[s].wait_recv()
        beyond = ext[s, pl.ds(tokens, 8)]
        ext[s, pl.ds(tokens, 8)] = jnp.where(me < n - 1, beyond, 0.0)
        out[...] = (
            short[s, 0:1, :] * ext[s, pl.ds(0, tokens)]
            + short[s, 1:2, :] * ext[s, pl.ds(1, tokens)]
            + short[s, 2:3, :] * ext[s, pl.ds(2, tokens)]
        ).astype(BF16)
    for edge in edges:
        edge.wait_send()
    for i in range(3):
        whole(me, n, send.at[i], recv.at[i], sems.at[i]).wait_send()


def vmem(count):
    return [pl.BlockSpec(memory_space=pltpu.VMEM)] * count


def body(query_in, key_in, value_in, short_filter, skip_gain, filter_taps, out_weight, out_grad):
    n = lax.axis_size("seq")
    tokens, channels = query_in.shape
    features = out_weight.shape[1]
    tabs = tables(n, tokens)
    bins = 8 * tabs[1].shape[1]
    gain = skip_gain[None]
    grads = lax.all_gather(out_grad, "tp", axis=0, tiled=True)
    block = lambda kind: jax.ShapeDtypeStruct((tokens, channels), kind)
    spectra = jax.ShapeDtypeStruct((bins, 2 * tokens), F32)
    scratch = [
        pltpu.VMEM((16 * n, LANES), F32),
        pltpu.VMEM((bins, 2 * tokens), F32),
        pltpu.VMEM((3, n, 16, LANES), BF16),
        pltpu.VMEM((3, n, 16, LANES), BF16),
        pltpu.SemaphoreType.DMA((2, 3)),
        pltpu.SemaphoreType.DMA((3, 2)),
    ]
    limit = 40 * 1024 * 1024
    q_short, k_short, v_short, response, gate, sig_spec, tap_spec = pl.pallas_call(
        functools.partial(front, n),
        out_shape=[block(BF16)] * 3 + [block(F32), block(BF16), spectra, spectra],
        in_specs=vmem(11),
        out_specs=vmem(7),
        scratch_shapes=[
            pltpu.VMEM((3, tokens + 8, channels), F32),
            pltpu.VMEM((3, 16, channels), BF16),
        ]
        + scratch,
        compiler_params=pltpu.CompilerParams(
            collective_id=0, has_side_effects=True, vmem_limit_bytes=limit
        ),
        name="front",
    )(query_in, key_in, value_in, filter_taps, short_filter, gain, *tabs)
    step = 512
    mixed_part, grad_gate = pl.pallas_call(
        project,
        grid=(features // step,),
        out_shape=[jax.ShapeDtypeStruct((tokens, features), BF16), block(F32)],
        in_specs=[
            pl.BlockSpec((tokens, channels), lambda i: (0, 0)),
            pl.BlockSpec((channels, step), lambda i: (0, i)),
            pl.BlockSpec((tokens, step), lambda i: (0, i)),
        ],
        out_specs=[
            pl.BlockSpec((tokens, step), lambda i: (0, i)),
            pl.BlockSpec((tokens, channels), lambda i: (0, 0)),
        ],
        compiler_params=pltpu.CompilerParams(vmem_limit_bytes=limit),
        name="project",
    )(gate, out_weight, grads)
    mixed_out = lax.psum_scatter(mixed_part, "tp", scatter_dimension=0, tiled=True)
    grad_query, grad_key, grad_value, filter_grad = pl.pallas_call(
        functools.partial(rear, n),
        out_shape=[block(BF16)] * 3 + [block(F32)],
        in_specs=vmem(14),
        out_specs=vmem(4),
        scratch_shapes=[
            pltpu.VMEM((3, tokens + 8, channels), F32),
            pltpu.VMEM((bins, 2 * tokens), F32),
        ]
        + scratch,
        compiler_params=pltpu.CompilerParams(
            collective_id=1, has_side_effects=True, vmem_limit_bytes=limit
        ),
        name="rear",
    )(q_short, k_short, v_short, response, grad_gate, short_filter, gain, sig_spec, tap_spec, *tabs)
    return (mixed_out, grad_query, grad_key, grad_value, filter_grad)


def solution(mesh):
    in_specs = (
        P("seq", "tp"),
        P("seq", "tp"),
        P("seq", "tp"),
        P(None, None, "tp"),
        P("tp"),
        P("seq", "tp"),
        P("tp", None),
        P(("seq", "tp"), None),
    )
    out_specs = (
        P(("seq", "tp"), None),
        P("seq", "tp"),
        P("seq", "tp"),
        P("seq", "tp"),
        P("seq", "tp"),
    )
    return jax.shard_map(body, mesh=mesh, in_specs=in_specs, out_specs=out_specs, check_vma=False)
```

```python
import functools
import math

import jax
import jax.numpy as jnp
import numpy as np
from jax import lax
from jax.experimental import pallas as pl
from jax.experimental.pallas import tpu as pltpu
from jax.sharding import PartitionSpec as P

MESH = pl.DeviceIdType.MESH
BF16, F32 = jnp.bfloat16, jnp.float32
LANES = 128


def tables(shards, rows):
    outer, full = 2 * shards, 2 * shards * rows
    half = outer // 2 + 1
    padded = -(-half // 8) * 8
    freq, shard, row = np.arange(half), np.arange(shards), np.arange(rows)
    outer_angle = 2 * np.pi * (freq[:, None] * shard[None] % outer) / outer
    twist_angle = 2 * np.pi * (freq[:, None] * row[None] % full) / full
    inner_angle = 2 * np.pi * (row[:, None] * row[None] % rows) / rows
    first = np.zeros((2 * padded, shards))
    first[:half], first[padded : padded + half] = np.cos(outer_angle), -np.sin(outer_angle)
    twist = np.zeros((2, padded, rows))
    twist[0, :half], twist[1, :half] = np.cos(twist_angle), -np.sin(twist_angle)
    cos, sin = np.cos(inner_angle), -np.sin(inner_angle)
    inner = np.block([[cos, sin], [-sin, cos]])
    weight = np.full((half, 1), 2.0 / full)
    weight[0] = weight[-1] = 1.0 / full
    last = np.zeros((shards, 2 * padded))
    last[:, :half] = (weight * np.cos(outer_angle)).T
    last[:, padded : padded + half] = -(weight * np.sin(outer_angle)).T
    as_bf16 = lambda a: jnp.asarray(a.astype(np.float32)).astype(BF16)
    return (
        as_bf16(first),
        jnp.asarray(twist.astype(np.float32)),
        as_bf16(inner),
        as_bf16(inner.T),
        as_bf16(last),
    )


def dot(a, b):
    return jnp.dot(a, b, preferred_element_type=F32)


def enter(n, m):
    me, part = lax.axis_index("seq"), lax.axis_index("tp")
    barrier = pltpu.get_barrier_semaphore()
    for axis, here, count in (("tp", part, m), ("seq", me, n)):

        def greet(i, carry):
            peer = lax.rem(here + i, count)
            pl.semaphore_signal(barrier, inc=1, device_id={axis: peer}, device_id_type=MESH)
            return carry

        lax.fori_loop(1, count, greet, 0)
    pl.semaphore_wait(barrier, n + m - 2)
    return me, part


def exchange_start(me, n, send, recv, sems):
    def push(i, carry):
        peer = lax.rem(me + i, n)
        pltpu.make_async_remote_copy(
            src_ref=send.at[peer],
            dst_ref=recv.at[me],
            send_sem=sems.at[0],
            recv_sem=sems.at[1],
            device_id={"seq": peer},
            device_id_type=MESH,
        ).start()
        return carry

    lax.fori_loop(1, n, push, 0)
    recv[pl.ds(me, 1)] = send[pl.ds(me, 1)]


def whole(me, n, send, recv, sems):
    return pltpu.make_async_remote_copy(
        src_ref=send.at[pl.ds(0, n - 1)],
        dst_ref=recv.at[pl.ds(0, n - 1)],
        send_sem=sems.at[0],
        recv_sem=sems.at[1],
        device_id={"seq": lax.rem(me + 1, n)},
        device_id_type=MESH,
    )


def pack(value, send, n):
    halves = [
        value[h * LANES : (h + 1) * LANES].T.reshape(n, 8, LANES) for h in range(2)
    ]
    send[...] = jnp.concatenate(halves, axis=1).astype(BF16)


def unpack(recv, n):
    value = recv[...].astype(F32)
    return jnp.concatenate(
        [value[:, 8 * h : 8 * h + 8].reshape(8 * n, LANES).T for h in range(2)], axis=0
    )


def spectrum(n, recv, tabs, rowed, mid, out):
    first, twist, inner = tabs[:3]
    padded = twist.shape[1]
    width = twist.shape[2]
    rowed[...] = recv[...].astype(F32).reshape(16 * n, LANES)
    for c in range(8):
        x = jnp.concatenate(
            [rowed[pl.ds(8 * h + c, n, stride=16), :] for h in range(2)], axis=1
        ).astype(BF16)
        a = dot(first[...], x)
        re, im = a[:padded], a[padded:]
        rows = pl.ds(c * padded, padded)
        mid[rows, :width] = re * twist[0] - im * twist[1]
        mid[rows, width:] = re * twist[1] + im * twist[0]
    out[...] = dot(mid[...].astype(BF16), inner[...])


def synthesis(n, tabs, rowed, mid, send):
    twist, back, last = tabs[1], tabs[3], tabs[4]
    padded = twist.shape[1]
    width = twist.shape[2]
    mid[...] = dot(mid[...].astype(BF16), back[...])
    for c in range(8):
        rows = pl.ds(c * padded, padded)
        re, im = mid[rows, :width], mid[rows, width:]
        turned = jnp.concatenate(
            [re * twist[0] + im * twist[1], im * twist[0] - re * twist[1]], axis=0
        ).astype(BF16)
        y = dot(last[...], turned)
        for h in range(2):
            rowed[pl.ds(8 * h + c, n, stride=16), :] = y[:, h * LANES : (h + 1) * LANES]
    send[...] = rowed[...].reshape(n, 16, LANES).astype(BF16)


def operator(
    n, m, query, key, value, taps_in, short_in, gain_in, weight_in, grad_in,
    first_in, twist_in, inner_in, back_in, last_in,
    mixed_out, query_out, key_out, value_out, taps_out,
    ext, parts, total, results, lags, streams, taps, short, gain, weight, grads, first, twist, inner, back, last,
    halo, beyond, shifted, k_short, v_short, q_short, response, grad_gate, mixed,
    tap_spec, sig_spec, grad_spec, rowed, mid, send, recv,
    load_sems, gather_sems, scatter_sems, halo_sems, beyond_sems, sems, store_sems,
):
    tabs = (first, twist, inner, back, last)
    tokens = query.shape[0]
    width = twist.shape[2]
    own = tokens // m
    chunks, chunk = mixed.shape[0], mixed.shape[2]
    part = lax.axis_index("tp")
    mine = pl.ds(pl.multiple_of(part * own, own), own)
    loads = {}
    for i, (name, source, target) in enumerate((
        ("taps", taps_in, taps),
        ("key", key, streams.at[1]),
        ("value", value, streams.at[2]),
        ("short", short_in, short),
        ("gain", gain_in, gain),
        ("query", query, streams.at[0]),
        ("first", first_in, first),
        ("twist", twist_in, twist),
        ("inner", inner_in, inner),
        ("back", back_in, back),
        ("last", last_in, last),
        ("grad", grad_in, grads.at[mine]),
        ("weight", weight_in, weight),
    )):
        loads[name] = pltpu.make_async_copy(source, target, load_sems.at[i])
        loads[name].start()
    me, part = enter(n, m)

    gathers = []
    for d in (2, 1, 3):
        gathers.append(
            pltpu.make_async_remote_copy(
                src_ref=grad_in,
                dst_ref=grads.at[mine],
                send_sem=gather_sems.at[0, d - 1],
                recv_sem=gather_sems.at[1, d - 1],
                device_id={"tp": lax.rem(part + d, m)},
                device_id_type=MESH,
            )
        )
        gathers[-1].start()
    edges = []
    for s, stream in enumerate((query, key, value)):
        edges.append(
            pltpu.make_async_remote_copy(
                src_ref=stream.at[pl.ds(tokens - 16, 16)],
                dst_ref=halo.at[s],
                send_sem=halo_sems.at[0, s],
                recv_sem=halo_sems.at[1, s],
                device_id={"seq": lax.rem(me + 1, n)},
                device_id_type=MESH,
            )
        )
        edges[-1].start()
    everything = [whole(me, n, send.at[i], recv.at[i], sems.at[i]) for i in range(6)]

    loads["taps"].wait()
    pack(taps[...], send.at[0], n)
    exchange_start(me, n, send.at[0], recv.at[0], sems.at[0])
    loads["short"].wait()
    loads["gain"].wait()

    def shorten(s, name):
        loads[name].wait()
        shifted[pl.ds(8, tokens)] = streams[s].astype(F32)
        edges[s].wait_recv()
        shifted[pl.ds(0, 8)] = jnp.where(me > 0, halo[s].astype(F32)[8:], 0.0)
        return (
            short[s, 0:1, :] * shifted[pl.ds(8, tokens)]
            + short[s, 1:2, :] * shifted[pl.ds(7, tokens)]
            + short[s, 2:3, :] * shifted[pl.ds(6, tokens)]
        ).astype(BF16)

    k_short[...] = shorten(1, "key")
    v_short[...] = shorten(2, "value")
    signal = k_short[...].astype(F32) * v_short[...].astype(F32)
    pack(signal, send.at[1], n)
    exchange_start(me, n, send.at[1], recv.at[1], sems.at[1])
    response[...] = gain[...] * signal
    q_short[...] = shorten(0, "query")
    for name in ("first", "twist", "inner", "back", "last"):
        loads[name].wait()
    everything[0].wait_recv()
    spectrum(n, recv.at[0], tabs, rowed, mid, tap_spec)
    everything[1].wait_recv()
    spectrum(n, recv.at[1], tabs, rowed, mid, sig_spec)
    ar, ai = tap_spec[:, :width], tap_spec[:, width:]
    br, bi = sig_spec[:, :width], sig_spec[:, width:]
    mid[:, :width] = ar * br - ai * bi
    mid[:, width:] = ar * bi + ai * br
    synthesis(n, tabs, rowed, mid, send.at[2])
    exchange_start(me, n, send.at[2], recv.at[2], sems.at[2])

    loads["grad"].wait()
    loads["weight"].wait()
    for gather in gathers:
        gather.wait_recv()
    grad_gate[...] = lax.dot_general(
        grads[...], weight[...], (((1,), (1,)), ((), ())), preferred_element_type=F32
    )
    pack(grad_gate[...] * q_short[...].astype(F32), send.at[3], n)
    exchange_start(me, n, send.at[3], recv.at[3], sems.at[3])

    everything[2].wait_recv()
    response[...] += unpack(recv.at[2], n)
    gate = (q_short[...].astype(F32) * response[...]).astype(BF16)
    scatters = []
    for j in range(chunks):
        mixed[j] = dot(gate, weight[:, j * chunk : (j + 1) * chunk]).astype(BF16)
        for d in (2, 1, 3):
            peer = lax.rem(part + d, m)
            scatters.append(
                pltpu.make_async_remote_copy(
                    src_ref=mixed.at[j, pl.ds(pl.multiple_of(peer * own, own), own)],
                    dst_ref=parts.at[part, j],
                    send_sem=scatter_sems.at[0, j, d - 1],
                    recv_sem=scatter_sems.at[1, j, d - 1],
                    device_id={"tp": peer},
                    device_id_type=MESH,
                )
            )
            scatters[-1].start()
        parts[part, j] = mixed[j, mine]

    forwards = [
        pltpu.make_async_remote_copy(
            src_ref=ext.at[s, pl.ds(0, 8)],
            dst_ref=beyond.at[s],
            send_sem=beyond_sems.at[0, s],
            recv_sem=beyond_sems.at[1, s],
            device_id={"seq": lax.rem(me + n - 1, n)},
            device_id_type=MESH,
        )
        for s in range(3)
    ]
    stores = [
        pltpu.make_async_copy(source, target, store_sems.at[i])
        for i, (source, target) in enumerate((
            (results.at[0], query_out),
            (results.at[1], key_out),
            (results.at[2], value_out),
            (lags, taps_out),
            (total, mixed_out),
        ))
    ]

    def lengthen(s):
        forwards[s].wait_recv()
        ext[s, pl.ds(tokens, 8)] = jnp.where(me < n - 1, beyond[s], 0.0)
        results[s] = (
            short[s, 0:1, :] * ext[s, pl.ds(0, tokens)]
            + short[s, 1:2, :] * ext[s, pl.ds(1, tokens)]
            + short[s, 2:3, :] * ext[s, pl.ds(2, tokens)]
        ).astype(BF16)
        stores[s].start()

    ext[0, pl.ds(0, tokens)] = grad_gate[...] * response[...]
    forwards[0].start()
    everything[3].wait_recv()
    spectrum(n, recv.at[3], tabs, rowed, mid, grad_spec)
    for i, other in ((4, tap_spec), (5, sig_spec)):
        ar, ai = other[:, :width], other[:, width:]
        br, bi = grad_spec[:, :width], grad_spec[:, width:]
        mid[:, :width] = ar * br + ai * bi
        mid[:, width:] = ar * bi - ai * br
        synthesis(n, tabs, rowed, mid, send.at[i])
        exchange_start(me, n, send.at[i], recv.at[i], sems.at[i])
    lengthen(0)
    grad_signal = gain[...] * (grad_gate[...] * q_short[...].astype(F32))
    everything[4].wait_recv()
    grad_signal += unpack(recv.at[4], n)
    ext[1, pl.ds(0, tokens)] = grad_signal * v_short[...].astype(F32)
    forwards[1].start()
    ext[2, pl.ds(0, tokens)] = grad_signal * k_short[...].astype(F32)
    forwards[2].start()
    everything[5].wait_recv()
    lags[...] = unpack(recv.at[5], n) * (1.0 / math.sqrt(tokens * n))
    stores[3].start()
    lengthen(1)
    lengthen(2)
    for scatter in scatters:
        scatter.wait_recv()
    for j in range(chunks):
        added = parts[0, j].astype(F32)
        for p in range(1, m):
            added += parts[p, j].astype(F32)
        total[:, j * chunk : (j + 1) * chunk] = added.astype(BF16)
    stores[4].start()
    for copy in gathers + edges + scatters + everything + forwards:
        copy.wait_send()
    for store in stores:
        store.wait()


def finish(*refs):
    sources, targets, sems = refs[:5], refs[5:10], refs[10]
    copies = [
        pltpu.make_async_copy(source, target, sems.at[i])
        for i, (source, target) in enumerate(zip(sources, targets))
    ]
    for copy in copies:
        copy.start()
    for copy in copies:
        copy.wait()


def hbm(count):
    return [pl.BlockSpec(memory_space=pltpu.HBM)] * count


def body(query_in, key_in, value_in, short_filter, skip_gain, filter_taps, out_weight, out_grad):
    n, m = lax.axis_size("seq"), lax.axis_size("tp")
    tokens, channels = query_in.shape
    features = out_weight.shape[1]
    tabs = tables(n, tokens)
    bins = 8 * tabs[1].shape[1]
    chunks = 4
    own = tokens // m
    kept = pltpu.VMEM
    outputs = (
        [jax.ShapeDtypeStruct((own, features), BF16)]
        + [jax.ShapeDtypeStruct((tokens, channels), BF16)] * 3
        + [jax.ShapeDtypeStruct((tokens, channels), F32)]
    )
    limit = pltpu.CompilerParams(
        collective_id=0, has_side_effects=True, vmem_limit_bytes=58 * 1024 * 1024
    )
    held = pl.pallas_call(
        functools.partial(operator, n, m),
        out_shape=outputs,
        in_specs=hbm(13),
        out_specs=hbm(5),
        scratch_shapes=[
            kept((3, tokens + 8, channels), F32),
            kept((m, chunks, own, features // chunks), BF16),
            kept((own, features), BF16),
            kept((3, tokens, channels), BF16),
            kept((tokens, channels), F32),
            kept((3, tokens, channels), BF16),
            kept((tokens, channels), F32),
            kept(short_filter.shape, F32),
            kept((1, channels), F32),
            kept(out_weight.shape, BF16),
            kept((tokens, features), BF16),
        ]
        + [kept(t.shape, t.dtype) for t in tabs]
        + [
            kept((3, 16, channels), BF16),
            kept((3, 8, channels), F32),
            kept((tokens + 8, channels), F32),
        ]
        + [kept((tokens, channels), BF16)] * 3
        + [kept((tokens, channels), F32)] * 2
        + [kept((chunks, tokens, features // chunks), BF16)]
        + [kept((bins, 2 * tokens), F32)] * 3
        + [
            kept((16 * n, LANES), F32),
            kept((bins, 2 * tokens), F32),
            kept((6, n, 16, LANES), BF16),
            kept((6, n, 16, LANES), BF16),
            pltpu.SemaphoreType.DMA((13,)),
            pltpu.SemaphoreType.DMA((2, m - 1)),
            pltpu.SemaphoreType.DMA((2, chunks, m - 1)),
            pltpu.SemaphoreType.DMA((2, 3)),
            pltpu.SemaphoreType.DMA((2, 3)),
            pltpu.SemaphoreType.DMA((6, 2)),
            pltpu.SemaphoreType.DMA((5,)),
        ],
        compiler_params=limit,
        name="operator",
    )(
        query_in, key_in, value_in, filter_taps, short_filter, skip_gain[None], out_weight,
        out_grad, *tabs,
    )
    return pl.pallas_call(
        finish,
        out_shape=outputs,
        in_specs=hbm(5),
        out_specs=hbm(5),
        scratch_shapes=[pltpu.SemaphoreType.DMA((5,))],
        compiler_params=pltpu.CompilerParams(vmem_limit_bytes=58 * 1024 * 1024),
        name="finish",
    )(*held)


def solution(mesh):
    in_specs = (
        P("seq", "tp"),
        P("seq", "tp"),
        P("seq", "tp"),
        P(None, None, "tp"),
        P("tp"),
        P("seq", "tp"),
        P("tp", None),
        P(("seq", "tp"), None),
    )
    out_specs = (
        P(("seq", "tp"), None),
        P("seq", "tp"),
        P("seq", "tp"),
        P("seq", "tp"),
        P("seq", "tp"),
    )
    return jax.shard_map(body, mesh=mesh, in_specs=in_specs, out_specs=out_specs, check_vma=False)
```

```python
import functools
import math

import jax
import jax.numpy as jnp
import numpy as np
from jax import lax
from jax.experimental import pallas as pl
from jax.experimental.pallas import tpu as pltpu
from jax.sharding import PartitionSpec as P

MESH = pl.DeviceIdType.MESH
BF16, F32 = jnp.bfloat16, jnp.float32
LANES = 128


def tables(shards, rows):
    outer, full = 2 * shards, 2 * shards * rows
    half = outer // 2 + 1
    padded = -(-half // 8) * 8
    freq, shard, row = np.arange(half), np.arange(shards), np.arange(rows)
    outer_angle = 2 * np.pi * (freq[:, None] * shard[None] % outer) / outer
    twist_angle = 2 * np.pi * (freq[:, None] * row[None] % full) / full
    inner_angle = 2 * np.pi * (row[:, None] * row[None] % rows) / rows
    first = np.zeros((2 * padded, shards))
    first[:half], first[padded : padded + half] = np.cos(outer_angle), -np.sin(outer_angle)
    twist = np.zeros((2, padded, rows))
    twist[0, :half], twist[1, :half] = np.cos(twist_angle), -np.sin(twist_angle)
    cos, sin = np.cos(inner_angle), -np.sin(inner_angle)
    inner = np.block([[cos, sin], [-sin, cos]])
    weight = np.full((half, 1), 2.0 / full)
    weight[0] = weight[-1] = 1.0 / full
    last = np.zeros((shards, 2 * padded))
    last[:, :half] = (weight * np.cos(outer_angle)).T
    last[:, padded : padded + half] = -(weight * np.sin(outer_angle)).T
    as_bf16 = lambda a: jnp.asarray(a.astype(np.float32)).astype(BF16)
    return (
        as_bf16(first),
        jnp.asarray(twist.astype(np.float32)),
        as_bf16(inner),
        as_bf16(inner.T),
        as_bf16(last),
    )


def dot(a, b):
    return jnp.dot(a, b, preferred_element_type=F32)


def enter(n, m):
    me, part = lax.axis_index("seq"), lax.axis_index("tp")
    barrier = pltpu.get_barrier_semaphore()
    for axis, here, count in (("tp", part, m), ("seq", me, n)):

        def greet(i, carry):
            peer = lax.rem(here + i, count)
            pl.semaphore_signal(barrier, inc=1, device_id={axis: peer}, device_id_type=MESH)
            return carry

        lax.fori_loop(1, count, greet, 0)
    pl.semaphore_wait(barrier, n + m - 2)
    return me, part


def exchange_start(me, n, send, recv, sems):
    def push(i, carry):
        peer = lax.rem(me + i, n)
        pltpu.make_async_remote_copy(
            src_ref=send.at[peer],
            dst_ref=recv.at[me],
            send_sem=sems.at[0],
            recv_sem=sems.at[1],
            device_id={"seq": peer},
            device_id_type=MESH,
        ).start()
        return carry

    lax.fori_loop(1, n, push, 0)
    recv[pl.ds(me, 1)] = send[pl.ds(me, 1)]


def whole(me, n, send, recv, sems):
    return pltpu.make_async_remote_copy(
        src_ref=send.at[pl.ds(0, n - 1)],
        dst_ref=recv.at[pl.ds(0, n - 1)],
        send_sem=sems.at[0],
        recv_sem=sems.at[1],
        device_id={"seq": lax.rem(me + 1, n)},
        device_id_type=MESH,
    )


def pack(value, send, n):
    halves = [
        value[h * LANES : (h + 1) * LANES].T.reshape(n, 8, LANES) for h in range(2)
    ]
    send[...] = jnp.concatenate(halves, axis=1).astype(BF16)


def unpack(recv, n):
    value = recv[...].astype(F32)
    return jnp.concatenate(
        [value[:, 8 * h : 8 * h + 8].reshape(8 * n, LANES).T for h in range(2)], axis=0
    )


def spectrum(n, recv, tabs, rowed, mid, out):
    first, twist, inner = tabs[:3]
    padded = twist.shape[1]
    width = twist.shape[2]
    rowed[...] = recv[...].astype(F32).reshape(16 * n, LANES)
    for c in range(8):
        x = jnp.concatenate(
            [rowed[pl.ds(8 * h + c, n, stride=16), :] for h in range(2)], axis=1
        ).astype(BF16)
        a = dot(first[...], x)
        re, im = a[:padded], a[padded:]
        rows = pl.ds(c * padded, padded)
        mid[rows, :width] = re * twist[0] - im * twist[1]
        mid[rows, width:] = re * twist[1] + im * twist[0]
    out[...] = dot(mid[...].astype(BF16), inner[...])


def synthesis(n, tabs, rowed, mid, send):
    twist, back, last = tabs[1], tabs[3], tabs[4]
    padded = twist.shape[1]
    width = twist.shape[2]
    mid[...] = dot(mid[...].astype(BF16), back[...])
    for c in range(8):
        rows = pl.ds(c * padded, padded)
        re, im = mid[rows, :width], mid[rows, width:]
        turned = jnp.concatenate(
            [re * twist[0] + im * twist[1], im * twist[0] - re * twist[1]], axis=0
        ).astype(BF16)
        y = dot(last[...], turned)
        for h in range(2):
            rowed[pl.ds(8 * h + c, n, stride=16), :] = y[:, h * LANES : (h + 1) * LANES]
    send[...] = rowed[...].reshape(n, 16, LANES).astype(BF16)


def operator(
    n, m, query, key, value, taps_in, short_in, gain_in, weight_in, grad_in,
    first_in, twist_in, inner_in, back_in, last_in,
    mixed_out, query_out, key_out, value_out, taps_out,
    ext, parts, total, results, lags, streams, taps, short, gain, weight, grads, first, twist, inner, back, last,
    halo, beyond, shifted, k_short, v_short, q_short, response, grad_gate, mixed,
    tap_spec, sig_spec, grad_spec, rowed, mid, send, recv,
    load_sems, gather_sems, scatter_sems, halo_sems, beyond_sems, sems, store_sems,
):
    tabs = (first, twist, inner, back, last)
    tokens = query.shape[0]
    width = twist.shape[2]
    own = tokens // m
    chunks, chunk = mixed.shape[0], mixed.shape[2]
    part = lax.axis_index("tp")
    mine = pl.ds(pl.multiple_of(part * own, own), own)
    loads = {}
    for i, (name, source, target) in enumerate((
        ("taps", taps_in, taps),
        ("key", key, streams.at[1]),
        ("value", value, streams.at[2]),
        ("short", short_in, short),
        ("gain", gain_in, gain),
        ("query", query, streams.at[0]),
        ("first", first_in, first),
        ("twist", twist_in, twist),
        ("inner", inner_in, inner),
        ("back", back_in, back),
        ("last", last_in, last),
        ("grad", grad_in, grads.at[mine]),
        ("weight", weight_in, weight),
    )):
        loads[name] = pltpu.make_async_copy(source, target, load_sems.at[i])
        loads[name].start()
    me, part = enter(n, m)

    gathers = []
    for d in (2, 1, 3):
        gathers.append(
            pltpu.make_async_remote_copy(
                src_ref=grad_in,
                dst_ref=grads.at[mine],
                send_sem=gather_sems.at[0, d - 1],
                recv_sem=gather_sems.at[1, d - 1],
                device_id={"tp": lax.rem(part + d, m)},
                device_id_type=MESH,
            )
        )
        gathers[-1].start()
    edges = []
    for s, stream in enumerate((query, key, value)):
        edges.append(
            pltpu.make_async_remote_copy(
                src_ref=stream.at[pl.ds(tokens - 16, 16)],
                dst_ref=halo.at[s],
                send_sem=halo_sems.at[0, s],
                recv_sem=halo_sems.at[1, s],
                device_id={"seq": lax.rem(me + 1, n)},
                device_id_type=MESH,
            )
        )
        edges[-1].start()
    everything = [whole(me, n, send.at[i], recv.at[i], sems.at[i]) for i in range(6)]

    loads["taps"].wait()
    pack(taps[...], send.at[0], n)
    exchange_start(me, n, send.at[0], recv.at[0], sems.at[0])
    loads["short"].wait()
    loads["gain"].wait()

    def shorten(s, name):
        loads[name].wait()
        shifted[pl.ds(8, tokens)] = streams[s].astype(F32)
        edges[s].wait_recv()
        shifted[pl.ds(0, 8)] = jnp.where(me > 0, halo[s].astype(F32)[8:], 0.0)
        return (
            short[s, 0:1, :] * shifted[pl.ds(8, tokens)]
            + short[s, 1:2, :] * shifted[pl.ds(7, tokens)]
            + short[s, 2:3, :] * shifted[pl.ds(6, tokens)]
        ).astype(BF16)

    k_short[...] = shorten(1, "key")
    v_short[...] = shorten(2, "value")
    signal = k_short[...].astype(F32) * v_short[...].astype(F32)
    pack(signal, send.at[1], n)
    exchange_start(me, n, send.at[1], recv.at[1], sems.at[1])
    response[...] = gain[...] * signal
    q_short[...] = shorten(0, "query")
    for name in ("first", "twist", "inner", "back", "last"):
        loads[name].wait()
    everything[0].wait_recv()
    spectrum(n, recv.at[0], tabs, rowed, mid, tap_spec)
    everything[1].wait_recv()
    spectrum(n, recv.at[1], tabs, rowed, mid, sig_spec)
    ar, ai = tap_spec[:, :width], tap_spec[:, width:]
    br, bi = sig_spec[:, :width], sig_spec[:, width:]
    mid[:, :width] = ar * br - ai * bi
    mid[:, width:] = ar * bi + ai * br
    synthesis(n, tabs, rowed, mid, send.at[2])
    exchange_start(me, n, send.at[2], recv.at[2], sems.at[2])

    loads["grad"].wait()
    loads["weight"].wait()
    for gather in gathers:
        gather.wait_recv()
    grad_gate[...] = lax.dot_general(
        grads[...], weight[...], (((1,), (1,)), ((), ())), preferred_element_type=F32
    )
    pack(grad_gate[...] * q_short[...].astype(F32), send.at[3], n)
    exchange_start(me, n, send.at[3], recv.at[3], sems.at[3])

    everything[2].wait_recv()
    response[...] += unpack(recv.at[2], n)
    gate = (q_short[...].astype(F32) * response[...]).astype(BF16)
    scatters = []
    for j in range(chunks):
        mixed[j] = dot(gate, weight[:, j * chunk : (j + 1) * chunk]).astype(BF16)
        for d in (2, 1, 3):
            peer = lax.rem(part + d, m)
            scatters.append(
                pltpu.make_async_remote_copy(
                    src_ref=mixed.at[j, pl.ds(pl.multiple_of(peer * own, own), own)],
                    dst_ref=parts.at[part, j],
                    send_sem=scatter_sems.at[0, j, d - 1],
                    recv_sem=scatter_sems.at[1, j, d - 1],
                    device_id={"tp": peer},
                    device_id_type=MESH,
                )
            )
            scatters[-1].start()
        parts[part, j] = mixed[j, mine]

    forwards = [
        pltpu.make_async_remote_copy(
            src_ref=ext.at[s, pl.ds(0, 8)],
            dst_ref=beyond.at[s],
            send_sem=beyond_sems.at[0, s],
            recv_sem=beyond_sems.at[1, s],
            device_id={"seq": lax.rem(me + n - 1, n)},
            device_id_type=MESH,
        )
        for s in range(3)
    ]
    stores = [
        pltpu.make_async_copy(source, target, store_sems.at[i])
        for i, (source, target) in enumerate((
            (results.at[0], query_out),
            (results.at[1], key_out),
            (results.at[2], value_out),
            (lags, taps_out),
            (total, mixed_out),
        ))
    ]

    def lengthen(s):
        forwards[s].wait_recv()
        ext[s, pl.ds(tokens, 8)] = jnp.where(me < n - 1, beyond[s], 0.0)
        results[s] = (
            short[s, 0:1, :] * ext[s, pl.ds(0, tokens)]
            + short[s, 1:2, :] * ext[s, pl.ds(1, tokens)]
            + short[s, 2:3, :] * ext[s, pl.ds(2, tokens)]
        ).astype(BF16)
        stores[s].start()

    ext[0, pl.ds(0, tokens)] = grad_gate[...] * response[...]
    forwards[0].start()
    everything[3].wait_recv()
    spectrum(n, recv.at[3], tabs, rowed, mid, grad_spec)
    for i, other in ((4, tap_spec), (5, sig_spec)):
        ar, ai = other[:, :width], other[:, width:]
        br, bi = grad_spec[:, :width], grad_spec[:, width:]
        mid[:, :width] = ar * br + ai * bi
        mid[:, width:] = ar * bi - ai * br
        synthesis(n, tabs, rowed, mid, send.at[i])
        exchange_start(me, n, send.at[i], recv.at[i], sems.at[i])
    lengthen(0)
    grad_signal = gain[...] * (grad_gate[...] * q_short[...].astype(F32))
    everything[4].wait_recv()
    grad_signal += unpack(recv.at[4], n)
    ext[1, pl.ds(0, tokens)] = grad_signal * v_short[...].astype(F32)
    forwards[1].start()
    ext[2, pl.ds(0, tokens)] = grad_signal * k_short[...].astype(F32)
    forwards[2].start()
    everything[5].wait_recv()
    lags[...] = unpack(recv.at[5], n) * (1.0 / math.sqrt(tokens * n))
    stores[3].start()
    lengthen(1)
    lengthen(2)
    for scatter in scatters:
        scatter.wait_recv()
    for j in range(chunks):
        added = parts[0, j].astype(F32)
        for p in range(1, m):
            added += parts[p, j].astype(F32)
        total[:, j * chunk : (j + 1) * chunk] = added.astype(BF16)
    stores[4].start()
    for copy in gathers + edges + scatters + everything + forwards:
        copy.wait_send()
    for store in stores:
        store.wait()


def finish(*refs):
    sources, targets, held, sems = refs[:5], refs[5:10], refs[10:15], refs[15]
    loads = [
        pltpu.make_async_copy(source, kept, sems.at[0, i])
        for i, (source, kept) in enumerate(zip(sources, held))
    ]
    stores = [
        pltpu.make_async_copy(kept, target, sems.at[1, i])
        for i, (kept, target) in enumerate(zip(held, targets))
    ]
    for load in loads:
        load.start()
    for load, store in zip(loads, stores):
        load.wait()
        store.start()
    for store in stores:
        store.wait()


def hbm(count):
    return [pl.BlockSpec(memory_space=pltpu.HBM)] * count


def body(query_in, key_in, value_in, short_filter, skip_gain, filter_taps, out_weight, out_grad):
    n, m = lax.axis_size("seq"), lax.axis_size("tp")
    tokens, channels = query_in.shape
    features = out_weight.shape[1]
    tabs = tables(n, tokens)
    bins = 8 * tabs[1].shape[1]
    chunks = 4
    own = tokens // m
    kept = pltpu.VMEM
    outputs = (
        [jax.ShapeDtypeStruct((own, features), BF16)]
        + [jax.ShapeDtypeStruct((tokens, channels), BF16)] * 3
        + [jax.ShapeDtypeStruct((tokens, channels), F32)]
    )
    limit = pltpu.CompilerParams(
        collective_id=0, has_side_effects=True, vmem_limit_bytes=58 * 1024 * 1024
    )
    held = pl.pallas_call(
        functools.partial(operator, n, m),
        out_shape=outputs,
        in_specs=hbm(13),
        out_specs=hbm(5),
        scratch_shapes=[
            kept((3, tokens + 8, channels), F32),
            kept((m, chunks, own, features // chunks), BF16),
            kept((own, features), BF16),
            kept((3, tokens, channels), BF16),
            kept((tokens, channels), F32),
            kept((3, tokens, channels), BF16),
            kept((tokens, channels), F32),
            kept(short_filter.shape, F32),
            kept((1, channels), F32),
            kept(out_weight.shape, BF16),
            kept((tokens, features), BF16),
        ]
        + [kept(t.shape, t.dtype) for t in tabs]
        + [
            kept((3, 16, channels), BF16),
            kept((3, 8, channels), F32),
            kept((tokens + 8, channels), F32),
        ]
        + [kept((tokens, channels), BF16)] * 3
        + [kept((tokens, channels), F32)] * 2
        + [kept((chunks, tokens, features // chunks), BF16)]
        + [kept((bins, 2 * tokens), F32)] * 3
        + [
            kept((16 * n, LANES), F32),
            kept((bins, 2 * tokens), F32),
            kept((6, n, 16, LANES), BF16),
            kept((6, n, 16, LANES), BF16),
            pltpu.SemaphoreType.DMA((13,)),
            pltpu.SemaphoreType.DMA((2, m - 1)),
            pltpu.SemaphoreType.DMA((2, chunks, m - 1)),
            pltpu.SemaphoreType.DMA((2, 3)),
            pltpu.SemaphoreType.DMA((2, 3)),
            pltpu.SemaphoreType.DMA((6, 2)),
            pltpu.SemaphoreType.DMA((5,)),
        ],
        compiler_params=limit,
        name="operator",
    )(
        query_in, key_in, value_in, filter_taps, short_filter, skip_gain[None], out_weight,
        out_grad, *tabs,
    )
    return pl.pallas_call(
        finish,
        out_shape=outputs,
        in_specs=hbm(5),
        out_specs=hbm(5),
        scratch_shapes=[kept(o.shape, o.dtype) for o in outputs]
        + [pltpu.SemaphoreType.DMA((2, 5))],
        compiler_params=pltpu.CompilerParams(vmem_limit_bytes=58 * 1024 * 1024),
        name="finish",
    )(*held)


def solution(mesh):
    in_specs = (
        P("seq", "tp"),
        P("seq", "tp"),
        P("seq", "tp"),
        P(None, None, "tp"),
        P("tp"),
        P("seq", "tp"),
        P("tp", None),
        P(("seq", "tp"), None),
    )
    out_specs = (
        P(("seq", "tp"), None),
        P("seq", "tp"),
        P("seq", "tp"),
        P("seq", "tp"),
        P("seq", "tp"),
    )
    return jax.shard_map(body, mesh=mesh, in_specs=in_specs, out_specs=out_specs, check_vma=False)
```

```python
import functools
import math

import jax
import jax.numpy as jnp
import numpy as np
from jax import lax
from jax.experimental import pallas as pl
from jax.experimental.pallas import tpu as pltpu
from jax.sharding import PartitionSpec as P

MESH = pl.DeviceIdType.MESH
BF16, F32 = jnp.bfloat16, jnp.float32
LANES = 128


def tables(shards, rows):
    outer, full = 2 * shards, 2 * shards * rows
    half = outer // 2 + 1
    padded = -(-half // 8) * 8
    freq, shard, row = np.arange(half), np.arange(shards), np.arange(rows)
    outer_angle = 2 * np.pi * (freq[:, None] * shard[None] % outer) / outer
    twist_angle = 2 * np.pi * (freq[:, None] * row[None] % full) / full
    inner_angle = 2 * np.pi * (row[:, None] * row[None] % rows) / rows
    first = np.zeros((2 * padded, shards))
    first[:half], first[padded : padded + half] = np.cos(outer_angle), -np.sin(outer_angle)
    twist = np.zeros((2, padded, rows))
    twist[0, :half], twist[1, :half] = np.cos(twist_angle), -np.sin(twist_angle)
    cos, sin = np.cos(inner_angle), -np.sin(inner_angle)
    inner = np.block([[cos, sin], [-sin, cos]])
    weight = np.full((half, 1), 2.0 / full)
    weight[0] = weight[-1] = 1.0 / full
    last = np.zeros((shards, 2 * padded))
    last[:, :half] = (weight * np.cos(outer_angle)).T
    last[:, padded : padded + half] = -(weight * np.sin(outer_angle)).T
    as_bf16 = lambda a: jnp.asarray(a.astype(np.float32)).astype(BF16)
    return (
        as_bf16(first),
        jnp.asarray(twist.astype(np.float32)),
        as_bf16(inner),
        as_bf16(inner.T),
        as_bf16(last),
    )


def dot(a, b):
    return jnp.dot(a, b, preferred_element_type=F32)


def announce(n, m):
    me, part = lax.axis_index("seq"), lax.axis_index("tp")
    barrier = pltpu.get_barrier_semaphore()
    for axis, here, count in (("tp", part, m), ("seq", me, n)):

        def greet(i, carry):
            peer = lax.rem(here + i, count)
            pl.semaphore_signal(barrier, inc=1, device_id={axis: peer}, device_id_type=MESH)
            return carry

        lax.fori_loop(1, count, greet, 0)
    return me, part


def exchange_start(me, n, send, recv, sems):
    def push(i, carry):
        peer = lax.rem(me + i, n)
        pltpu.make_async_remote_copy(
            src_ref=send.at[peer],
            dst_ref=recv.at[me],
            send_sem=sems.at[0],
            recv_sem=sems.at[1],
            device_id={"seq": peer},
            device_id_type=MESH,
        ).start()
        return carry

    lax.fori_loop(1, n, push, 0)
    recv[pl.ds(me, 1)] = send[pl.ds(me, 1)]


def whole(me, n, send, recv, sems):
    return pltpu.make_async_remote_copy(
        src_ref=send.at[pl.ds(0, n - 1)],
        dst_ref=recv.at[pl.ds(0, n - 1)],
        send_sem=sems.at[0],
        recv_sem=sems.at[1],
        device_id={"seq": lax.rem(me + 1, n)},
        device_id_type=MESH,
    )


def pack(value, send, n):
    halves = [
        value[h * LANES : (h + 1) * LANES].T.reshape(n, 8, LANES) for h in range(2)
    ]
    send[...] = jnp.concatenate(halves, axis=1).astype(BF16)


def unpack(recv, n):
    value = recv[...].astype(F32)
    return jnp.concatenate(
        [value[:, 8 * h : 8 * h + 8].reshape(8 * n, LANES).T for h in range(2)], axis=0
    )


def spectrum(n, recv, tabs, rowed, mid, out):
    first, twist, inner = tabs[:3]
    padded = twist.shape[1]
    width = twist.shape[2]
    rowed[...] = recv[...].astype(F32).reshape(16 * n, LANES)
    for c in range(8):
        x = jnp.concatenate(
            [rowed[pl.ds(8 * h + c, n, stride=16), :] for h in range(2)], axis=1
        ).astype(BF16)
        a = dot(first[...], x)
        re, im = a[:padded], a[padded:]
        rows = pl.ds(c * padded, padded)
        mid[rows, :width] = re * twist[0] - im * twist[1]
        mid[rows, width:] = re * twist[1] + im * twist[0]
    out[...] = dot(mid[...].astype(BF16), inner[...])


def synthesis(n, tabs, rowed, mid, send):
    twist, back, last = tabs[1], tabs[3], tabs[4]
    padded = twist.shape[1]
    width = twist.shape[2]
    mid[...] = dot(mid[...].astype(BF16), back[...])
    for c in range(8):
        rows = pl.ds(c * padded, padded)
        re, im = mid[rows, :width], mid[rows, width:]
        turned = jnp.concatenate(
            [re * twist[0] + im * twist[1], im * twist[0] - re * twist[1]], axis=0
        ).astype(BF16)
        y = dot(last[...], turned)
        for h in range(2):
            rowed[pl.ds(8 * h + c, n, stride=16), :] = y[:, h * LANES : (h + 1) * LANES]
    send[...] = rowed[...].reshape(n, 16, LANES).astype(BF16)


def operator(
    n, m, query, key, value, taps_in, short_in, gain_in, weight_in, grad_in,
    first_in, twist_in, inner_in, back_in, last_in,
    mixed_out, query_out, key_out, value_out, taps_out,
    ext, parts, relayed, summed, total, results, lags, streams, taps, short, gain, weight, grads, first, twist, inner, back, last,
    halo, beyond, shifted, k_short, v_short, q_short, response, grad_gate, mixed,
    tap_spec, sig_spec, grad_spec, rowed, mid, send, recv,
    load_sems, gather_sems, scatter_sems, halo_sems, beyond_sems, sems, store_sems,
):
    tabs = (first, twist, inner, back, last)
    tokens = query.shape[0]
    width = twist.shape[2]
    own = tokens // m
    chunks, chunk = mixed.shape[0], mixed.shape[2]
    me, part = announce(n, m)
    left, right, far = (lax.rem(part + d, m) for d in (3, 1, 2))
    mine = pl.ds(pl.multiple_of(part * own, own), own)
    loads = {}
    for i, (name, source, target) in enumerate((
        ("taps", taps_in, taps),
        ("key", key, streams.at[1]),
        ("value", value, streams.at[2]),
        ("short", short_in, short),
        ("gain", gain_in, gain),
        ("query", query, streams.at[0]),
        ("first", first_in, first),
        ("twist", twist_in, twist),
        ("inner", inner_in, inner),
        ("back", back_in, back),
        ("last", last_in, last),
        ("grad", grad_in, grads.at[mine]),
        ("weight", weight_in, weight),
    )):
        loads[name] = pltpu.make_async_copy(source, target, load_sems.at[i])
        loads[name].start()
    loads["taps"].wait()
    pack(taps[...], send.at[0], n)
    pl.semaphore_wait(pltpu.get_barrier_semaphore(), n + m - 2)

    def slab(owner, h):
        start = owner * own + h * (own // 2)
        return grads.at[pl.ds(pl.multiple_of(start, own // 2), own // 2)]

    def gather(k, source, owner, h, peer):
        return pltpu.make_async_remote_copy(
            src_ref=source,
            dst_ref=slab(owner, h),
            send_sem=gather_sems.at[0, k],
            recv_sem=gather_sems.at[1, k],
            device_id={"tp": peer},
            device_id_type=MESH,
        )

    halves = [grad_in.at[pl.ds(h * (own // 2), own // 2)] for h in range(2)]
    gathers = [
        gather(0, halves[1], part, 1, right),
        gather(1, halves[0], part, 0, left),
        gather(2, halves[0], part, 0, right),
        gather(3, halves[1], part, 1, left),
    ]
    passed = [
        gather(4, slab(left, 1), left, 1, right),
        gather(5, slab(right, 0), right, 0, left),
    ]
    for copy in gathers:
        copy.start()
    edges = []
    for s, stream in enumerate((query, key, value)):
        edges.append(
            pltpu.make_async_remote_copy(
                src_ref=stream.at[pl.ds(tokens - 16, 16)],
                dst_ref=halo.at[s],
                send_sem=halo_sems.at[0, s],
                recv_sem=halo_sems.at[1, s],
                device_id={"seq": lax.rem(me + 1, n)},
                device_id_type=MESH,
            )
        )
        edges[-1].start()
    everything = [whole(me, n, send.at[i], recv.at[i], sems.at[i]) for i in range(6)]

    exchange_start(me, n, send.at[0], recv.at[0], sems.at[0])
    loads["short"].wait()
    loads["gain"].wait()

    def shorten(s, name):
        loads[name].wait()
        shifted[pl.ds(8, tokens)] = streams[s].astype(F32)
        edges[s].wait_recv()
        shifted[pl.ds(0, 8)] = jnp.where(me > 0, halo[s].astype(F32)[8:], 0.0)
        return (
            short[s, 0:1, :] * shifted[pl.ds(8, tokens)]
            + short[s, 1:2, :] * shifted[pl.ds(7, tokens)]
            + short[s, 2:3, :] * shifted[pl.ds(6, tokens)]
        ).astype(BF16)

    k_short[...] = shorten(1, "key")
    v_short[...] = shorten(2, "value")
    signal = k_short[...].astype(F32) * v_short[...].astype(F32)
    pack(signal, send.at[1], n)
    exchange_start(me, n, send.at[1], recv.at[1], sems.at[1])
    response[...] = gain[...] * signal
    q_short[...] = shorten(0, "query")
    for name in ("first", "twist", "inner", "back", "last"):
        loads[name].wait()
    everything[0].wait_recv()
    spectrum(n, recv.at[0], tabs, rowed, mid, tap_spec)
    for arrived, copy in zip(gathers[:2], passed):
        arrived.wait_recv()
        copy.start()
    everything[1].wait_recv()
    spectrum(n, recv.at[1], tabs, rowed, mid, sig_spec)
    ar, ai = tap_spec[:, :width], tap_spec[:, width:]
    br, bi = sig_spec[:, :width], sig_spec[:, width:]
    mid[:, :width] = ar * br - ai * bi
    mid[:, width:] = ar * bi + ai * br
    synthesis(n, tabs, rowed, mid, send.at[2])
    exchange_start(me, n, send.at[2], recv.at[2], sems.at[2])

    loads["grad"].wait()
    loads["weight"].wait()
    for copy in gathers[2:] + passed:
        copy.wait_recv()
    grad_gate[...] = lax.dot_general(
        grads[...], weight[...], (((1,), (1,)), ((), ())), preferred_element_type=F32
    )
    pack(grad_gate[...] * q_short[...].astype(F32), send.at[3], n)
    exchange_start(me, n, send.at[3], recv.at[3], sems.at[3])

    everything[2].wait_recv()
    response[...] += unpack(recv.at[2], n)
    gate = (q_short[...].astype(F32) * response[...]).astype(BF16)

    def block(j, owner):
        return mixed.at[j, pl.ds(pl.multiple_of(owner * own, own), own)]

    def scatter(k, j, source, target, peer):
        return pltpu.make_async_remote_copy(
            src_ref=source,
            dst_ref=target,
            send_sem=scatter_sems.at[0, j, k],
            recv_sem=scatter_sems.at[1, j, k],
            device_id={"tp": peer},
            device_id_type=MESH,
        )

    ways = [(left, right, 1) if j < chunks // 2 else (right, left, 0) for j in range(chunks)]
    relays, directs, sums = [], [], []
    for j, (way, other, side) in enumerate(ways):
        relays.append(scatter(0, j, block(j, far), relayed.at[j], way))
        directs.append(scatter(1, j, block(j, other), parts.at[1 - side, j], other))
        sums.append(scatter(2, j, summed.at[j], parts.at[side, j], way))
    order = [j + h * (chunks // 2) for j in range(chunks // 2) for h in range(2)]
    for j in order:
        mixed[j] = dot(gate, weight[:, j * chunk : (j + 1) * chunk]).astype(BF16)
        relays[j].start()
        directs[j].start()

    forwards = [
        pltpu.make_async_remote_copy(
            src_ref=ext.at[s, pl.ds(0, 8)],
            dst_ref=beyond.at[s],
            send_sem=beyond_sems.at[0, s],
            recv_sem=beyond_sems.at[1, s],
            device_id={"seq": lax.rem(me + n - 1, n)},
            device_id_type=MESH,
        )
        for s in range(3)
    ]
    stores = [
        pltpu.make_async_copy(source, target, store_sems.at[i])
        for i, (source, target) in enumerate((
            (results.at[0], query_out),
            (results.at[1], key_out),
            (results.at[2], value_out),
            (lags, taps_out),
            (total, mixed_out),
        ))
    ]

    def lengthen(s):
        forwards[s].wait_recv()
        ext[s, pl.ds(tokens, 8)] = jnp.where(me < n - 1, beyond[s], 0.0)
        results[s] = (
            short[s, 0:1, :] * ext[s, pl.ds(0, tokens)]
            + short[s, 1:2, :] * ext[s, pl.ds(1, tokens)]
            + short[s, 2:3, :] * ext[s, pl.ds(2, tokens)]
        ).astype(BF16)
        stores[s].start()

    ext[0, pl.ds(0, tokens)] = grad_gate[...] * response[...]
    forwards[0].start()
    everything[3].wait_recv()
    spectrum(n, recv.at[3], tabs, rowed, mid, grad_spec)
    for i, other in ((4, tap_spec), (5, sig_spec)):
        ar, ai = other[:, :width], other[:, width:]
        br, bi = grad_spec[:, :width], grad_spec[:, width:]
        mid[:, :width] = ar * br + ai * bi
        mid[:, width:] = ar * bi - ai * br
        synthesis(n, tabs, rowed, mid, send.at[i])
        exchange_start(me, n, send.at[i], recv.at[i], sems.at[i])
    for j in order:
        relays[j].wait_recv()
        own_term = block(j, ways[j][0])[...].astype(F32)
        summed[j] = (own_term + relayed[j].astype(F32)).astype(BF16)
        sums[j].start()
    lengthen(0)
    grad_signal = gain[...] * (grad_gate[...] * q_short[...].astype(F32))
    everything[4].wait_recv()
    grad_signal += unpack(recv.at[4], n)
    ext[1, pl.ds(0, tokens)] = grad_signal * v_short[...].astype(F32)
    forwards[1].start()
    ext[2, pl.ds(0, tokens)] = grad_signal * k_short[...].astype(F32)
    forwards[2].start()
    everything[5].wait_recv()
    lags[...] = unpack(recv.at[5], n) * (1.0 / math.sqrt(tokens * n))
    stores[3].start()
    lengthen(1)
    lengthen(2)
    for j in order:
        directs[j].wait_recv()
        sums[j].wait_recv()
        added = parts[0, j].astype(F32) + parts[1, j].astype(F32)
        added += block(j, part)[...].astype(F32)
        total[:, j * chunk : (j + 1) * chunk] = added.astype(BF16)
    stores[4].start()
    for copy in gathers + passed + edges + relays + directs + sums + everything + forwards:
        copy.wait_send()
    for store in stores:
        store.wait()


def finish(*refs):
    sources, targets, held, sems = refs[:5], refs[5:10], refs[10:15], refs[15]
    loads = [
        pltpu.make_async_copy(source, kept, sems.at[0, i])
        for i, (source, kept) in enumerate(zip(sources, held))
    ]
    stores = [
        pltpu.make_async_copy(kept, target, sems.at[1, i])
        for i, (kept, target) in enumerate(zip(held, targets))
    ]
    for load in loads:
        load.start()
    for load, store in zip(loads, stores):
        load.wait()
        store.start()
    for store in stores:
        store.wait()


def hbm(count):
    return [pl.BlockSpec(memory_space=pltpu.HBM)] * count


def body(query_in, key_in, value_in, short_filter, skip_gain, filter_taps, out_weight, out_grad):
    n, m = lax.axis_size("seq"), lax.axis_size("tp")
    tokens, channels = query_in.shape
    features = out_weight.shape[1]
    tabs = tables(n, tokens)
    bins = 8 * tabs[1].shape[1]
    chunks = 4
    own = tokens // m
    kept = pltpu.VMEM
    outputs = (
        [jax.ShapeDtypeStruct((own, features), BF16)]
        + [jax.ShapeDtypeStruct((tokens, channels), BF16)] * 3
        + [jax.ShapeDtypeStruct((tokens, channels), F32)]
    )
    limit = pltpu.CompilerParams(
        collective_id=0, has_side_effects=True, vmem_limit_bytes=58 * 1024 * 1024
    )
    held = pl.pallas_call(
        functools.partial(operator, n, m),
        out_shape=outputs,
        in_specs=hbm(13),
        out_specs=hbm(5),
        scratch_shapes=[
            kept((3, tokens + 8, channels), F32),
            kept((2, chunks, own, features // chunks), BF16),
            kept((chunks, own, features // chunks), BF16),
            kept((chunks, own, features // chunks), BF16),
            kept((own, features), BF16),
            kept((3, tokens, channels), BF16),
            kept((tokens, channels), F32),
            kept((3, tokens, channels), BF16),
            kept((tokens, channels), F32),
            kept(short_filter.shape, F32),
            kept((1, channels), F32),
            kept(out_weight.shape, BF16),
            kept((tokens, features), BF16),
        ]
        + [kept(t.shape, t.dtype) for t in tabs]
        + [
            kept((3, 16, channels), BF16),
            kept((3, 8, channels), F32),
            kept((tokens + 8, channels), F32),
        ]
        + [kept((tokens, channels), BF16)] * 3
        + [kept((tokens, channels), F32)] * 2
        + [kept((chunks, tokens, features // chunks), BF16)]
        + [kept((bins, 2 * tokens), F32)] * 3
        + [
            kept((16 * n, LANES), F32),
            kept((bins, 2 * tokens), F32),
            kept((6, n, 16, LANES), BF16),
            kept((6, n, 16, LANES), BF16),
            pltpu.SemaphoreType.DMA((13,)),
            pltpu.SemaphoreType.DMA((2, 6)),
            pltpu.SemaphoreType.DMA((2, chunks, 3)),
            pltpu.SemaphoreType.DMA((2, 3)),
            pltpu.SemaphoreType.DMA((2, 3)),
            pltpu.SemaphoreType.DMA((6, 2)),
            pltpu.SemaphoreType.DMA((5,)),
        ],
        compiler_params=limit,
        name="operator",
    )(
        query_in, key_in, value_in, filter_taps, short_filter, skip_gain[None], out_weight,
        out_grad, *tabs,
    )
    return pl.pallas_call(
        finish,
        out_shape=outputs,
        in_specs=hbm(5),
        out_specs=hbm(5),
        scratch_shapes=[kept(o.shape, o.dtype) for o in outputs]
        + [pltpu.SemaphoreType.DMA((2, 5))],
        compiler_params=pltpu.CompilerParams(vmem_limit_bytes=58 * 1024 * 1024),
        name="finish",
    )(*held)


def solution(mesh):
    in_specs = (
        P("seq", "tp"),
        P("seq", "tp"),
        P("seq", "tp"),
        P(None, None, "tp"),
        P("tp"),
        P("seq", "tp"),
        P("tp", None),
        P(("seq", "tp"), None),
    )
    out_specs = (
        P(("seq", "tp"), None),
        P("seq", "tp"),
        P("seq", "tp"),
        P("seq", "tp"),
        P("seq", "tp"),
    )
    return jax.shard_map(body, mesh=mesh, in_specs=in_specs, out_specs=out_specs, check_vma=False)
```

```python
import functools
import math

import jax
import jax.numpy as jnp
import numpy as np
from jax import lax
from jax.experimental import pallas as pl
from jax.experimental.pallas import tpu as pltpu
from jax.sharding import PartitionSpec as P

MESH = pl.DeviceIdType.MESH
BF16, F32 = jnp.bfloat16, jnp.float32
LANES = 128


def tables(shards, rows):
    outer, full = 2 * shards, 2 * shards * rows
    half = outer // 2 + 1
    padded = -(-half // 8) * 8
    freq, shard, row = np.arange(half), np.arange(shards), np.arange(rows)
    outer_angle = 2 * np.pi * (freq[:, None] * shard[None] % outer) / outer
    twist_angle = 2 * np.pi * (freq[:, None] * row[None] % full) / full
    inner_angle = 2 * np.pi * (row[:, None] * row[None] % rows) / rows
    first = np.zeros((2 * padded, shards))
    first[:half], first[padded : padded + half] = np.cos(outer_angle), -np.sin(outer_angle)
    twist = np.zeros((2, padded, rows))
    twist[0, :half], twist[1, :half] = np.cos(twist_angle), -np.sin(twist_angle)
    cos, sin = np.cos(inner_angle), -np.sin(inner_angle)
    inner = np.block([[cos, sin], [-sin, cos]])
    weight = np.full((half, 1), 2.0 / full)
    weight[0] = weight[-1] = 1.0 / full
    last = np.zeros((shards, 2 * padded))
    last[:, :half] = (weight * np.cos(outer_angle)).T
    last[:, padded : padded + half] = -(weight * np.sin(outer_angle)).T
    as_bf16 = lambda a: jnp.asarray(a.astype(np.float32)).astype(BF16)
    return (
        as_bf16(first),
        jnp.asarray(twist.astype(np.float32)),
        as_bf16(inner),
        as_bf16(inner.T),
        as_bf16(last),
    )


def dot(a, b):
    return jnp.dot(a, b, preferred_element_type=F32)


def announce(n, m):
    me, part = lax.axis_index("seq"), lax.axis_index("tp")
    barrier = pltpu.get_barrier_semaphore()
    for axis, here, count in (("tp", part, m), ("seq", me, n)):

        def greet(i, carry):
            peer = lax.rem(here + i, count)
            pl.semaphore_signal(barrier, inc=1, device_id={axis: peer}, device_id_type=MESH)
            return carry

        lax.fori_loop(1, count, greet, 0)
    return me, part


def exchange_start(me, n, send, recv, sems, groups=(0, 1), keep=True):
    for group in groups:
        odd = lax.rem(me + group, 2)

        def push(i, carry):
            peer = lax.rem(me + 2 * i + odd, n)
            pltpu.make_async_remote_copy(
                src_ref=send.at[peer],
                dst_ref=recv.at[me],
                send_sem=sems.at[0],
                recv_sem=sems.at[1],
                device_id={"seq": peer},
                device_id_type=MESH,
            ).start()
            return carry

        lax.fori_loop(1 - odd, n // 2, push, 0)
    if keep and 0 in groups:
        recv[pl.ds(me, 1)] = send[pl.ds(me, 1)]


def whole(me, n, send, recv, sems):
    return pltpu.make_async_remote_copy(
        src_ref=send.at[pl.ds(0, n - 1)],
        dst_ref=recv.at[pl.ds(0, n - 1)],
        send_sem=sems.at[0],
        recv_sem=sems.at[1],
        device_id={"seq": lax.rem(me + 1, n)},
        device_id_type=MESH,
    )


def pack(value, send, n):
    halves = [
        value[h * LANES : (h + 1) * LANES].T.reshape(n, 8, LANES) for h in range(2)
    ]
    send[...] = jnp.concatenate(halves, axis=1).astype(BF16)


def unpack(recv, n):
    value = recv[...].astype(F32)
    return jnp.concatenate(
        [value[:, 8 * h : 8 * h + 8].reshape(8 * n, LANES).T for h in range(2)], axis=0
    )


def spectrum(n, recv, tabs, rowed, mid, out):
    first, twist, inner = tabs[:3]
    padded = twist.shape[1]
    width = twist.shape[2]
    rowed[...] = recv[...].astype(F32).reshape(16 * n, LANES)
    for c in range(8):
        x = jnp.concatenate(
            [rowed[pl.ds(8 * h + c, n, stride=16), :] for h in range(2)], axis=1
        ).astype(BF16)
        a = dot(first[...], x)
        re, im = a[:padded], a[padded:]
        rows = pl.ds(c * padded, padded)
        mid[rows, :width] = re * twist[0] - im * twist[1]
        mid[rows, width:] = re * twist[1] + im * twist[0]
    out[...] = dot(mid[...].astype(BF16), inner[...])


def synthesis(n, tabs, rowed, mid, send):
    twist, back, last = tabs[1], tabs[3], tabs[4]
    padded = twist.shape[1]
    width = twist.shape[2]
    mid[...] = dot(mid[...].astype(BF16), back[...])
    for c in range(8):
        rows = pl.ds(c * padded, padded)
        re, im = mid[rows, :width], mid[rows, width:]
        turned = jnp.concatenate(
            [re * twist[0] + im * twist[1], im * twist[0] - re * twist[1]], axis=0
        ).astype(BF16)
        y = dot(last[...], turned)
        for h in range(2):
            rowed[pl.ds(8 * h + c, n, stride=16), :] = y[:, h * LANES : (h + 1) * LANES]
    send[...] = rowed[...].reshape(n, 16, LANES).astype(BF16)


def operator(
    n, m, query, key, value, taps_in, short_in, gain_in, weight_in, grad_in,
    first_in, twist_in, inner_in, back_in, last_in,
    mixed_out, query_out, key_out, value_out, lags,
    ext, parts, relayed, summed, total, results, streams, taps, short, gain, weight, grads, first, twist, inner, back, last,
    halo, beyond, shifted, k_short, v_short, q_short, response, grad_gate, mixed,
    tap_spec, sig_spec, grad_spec, rowed, mid, send, recv,
    load_sems, gather_sems, scatter_sems, halo_sems, beyond_sems, sems, store_sems,
):
    tabs = (first, twist, inner, back, last)
    tokens = query.shape[0]
    width = twist.shape[2]
    own = tokens // m
    chunks, chunk = mixed.shape[0], mixed.shape[2]
    me, part = announce(n, m)
    left, right, far = (lax.rem(part + d, m) for d in (3, 1, 2))
    mine = pl.ds(pl.multiple_of(part * own, own), own)
    loads = {}
    for i, (name, source, target) in enumerate((
        ("taps", taps_in, taps),
        ("key", key, streams.at[1]),
        ("value", value, streams.at[2]),
        ("short", short_in, short),
        ("gain", gain_in, gain),
        ("query", query, streams.at[0]),
        ("first", first_in, first),
        ("twist", twist_in, twist),
        ("inner", inner_in, inner),
        ("back", back_in, back),
        ("last", last_in, last),
        ("grad", grad_in, grads.at[mine]),
        ("weight", weight_in, weight),
    )):
        loads[name] = pltpu.make_async_copy(source, target, load_sems.at[i])
        loads[name].start()
    loads["taps"].wait()
    pack(taps[...], send.at[0], n)
    pl.semaphore_wait(pltpu.get_barrier_semaphore(), n + m - 2)

    def slab(owner, h):
        start = owner * own + h * (own // 2)
        return grads.at[pl.ds(pl.multiple_of(start, own // 2), own // 2)]

    def gather(k, source, owner, h, peer):
        return pltpu.make_async_remote_copy(
            src_ref=source,
            dst_ref=slab(owner, h),
            send_sem=gather_sems.at[0, k],
            recv_sem=gather_sems.at[1, k],
            device_id={"tp": peer},
            device_id_type=MESH,
        )

    halves = [grad_in.at[pl.ds(h * (own // 2), own // 2)] for h in range(2)]
    gathers = [
        gather(0, halves[1], part, 1, right),
        gather(1, halves[0], part, 0, left),
        gather(2, halves[0], part, 0, right),
        gather(3, halves[1], part, 1, left),
    ]
    passed = [
        gather(4, slab(left, 1), left, 1, right),
        gather(5, slab(right, 0), right, 0, left),
    ]
    for copy in gathers[:2]:
        copy.start()
    edges = []
    for s, stream in enumerate((query, key, value)):
        edges.append(
            pltpu.make_async_remote_copy(
                src_ref=stream.at[pl.ds(tokens - 16, 16)],
                dst_ref=halo.at[s],
                send_sem=halo_sems.at[0, s],
                recv_sem=halo_sems.at[1, s],
                device_id={"seq": lax.rem(me + 1, n)},
                device_id_type=MESH,
            )
        )
        edges[-1].start()
    landing = [recv.at[i] for i in range(5)] + [lags]
    everything = [whole(me, n, send.at[i], landing[i], sems.at[i]) for i in range(6)]

    exchange_start(me, n, send.at[0], recv.at[0], sems.at[0], (0,))
    loads["short"].wait()
    loads["gain"].wait()

    def shorten(s, name):
        loads[name].wait()
        shifted[pl.ds(8, tokens)] = streams[s].astype(F32)
        edges[s].wait_recv()
        shifted[pl.ds(0, 8)] = jnp.where(me > 0, halo[s].astype(F32)[8:], 0.0)
        return (
            short[s, 0:1, :] * shifted[pl.ds(8, tokens)]
            + short[s, 1:2, :] * shifted[pl.ds(7, tokens)]
            + short[s, 2:3, :] * shifted[pl.ds(6, tokens)]
        ).astype(BF16)

    k_short[...] = shorten(1, "key")
    v_short[...] = shorten(2, "value")
    signal = k_short[...].astype(F32) * v_short[...].astype(F32)
    pack(signal, send.at[1], n)
    exchange_start(me, n, send.at[1], recv.at[1], sems.at[1], (0,))
    exchange_start(me, n, send.at[0], recv.at[0], sems.at[0], (1,))
    exchange_start(me, n, send.at[1], recv.at[1], sems.at[1], (1,))
    for copy in gathers[2:]:
        copy.start()
    response[...] = gain[...] * signal
    q_short[...] = shorten(0, "query")
    for name in ("first", "twist", "inner", "back", "last"):
        loads[name].wait()
    everything[0].wait_recv()
    spectrum(n, recv.at[0], tabs, rowed, mid, tap_spec)
    for arrived, copy in zip(gathers[:2], passed):
        arrived.wait_recv()
        copy.start()
    everything[1].wait_recv()
    spectrum(n, recv.at[1], tabs, rowed, mid, sig_spec)
    ar, ai = tap_spec[:, :width], tap_spec[:, width:]
    br, bi = sig_spec[:, :width], sig_spec[:, width:]
    mid[:, :width] = ar * br - ai * bi
    mid[:, width:] = ar * bi + ai * br
    synthesis(n, tabs, rowed, mid, send.at[2])
    exchange_start(me, n, send.at[2], recv.at[2], sems.at[2])

    loads["grad"].wait()
    loads["weight"].wait()
    for copy in gathers[2:] + passed:
        copy.wait_recv()
    grad_gate[...] = lax.dot_general(
        grads[...], weight[...], (((1,), (1,)), ((), ())), preferred_element_type=F32
    )
    pack(grad_gate[...] * q_short[...].astype(F32), send.at[3], n)
    exchange_start(me, n, send.at[3], recv.at[3], sems.at[3])

    everything[2].wait_recv()
    response[...] += unpack(recv.at[2], n)
    gate = (q_short[...].astype(F32) * response[...]).astype(BF16)

    def block(j, owner):
        return mixed.at[j, pl.ds(pl.multiple_of(owner * own, own), own)]

    def scatter(k, j, source, target, peer):
        return pltpu.make_async_remote_copy(
            src_ref=source,
            dst_ref=target,
            send_sem=scatter_sems.at[0, j, k],
            recv_sem=scatter_sems.at[1, j, k],
            device_id={"tp": peer},
            device_id_type=MESH,
        )

    ways = [(left, right, 1) if j < chunks // 2 else (right, left, 0) for j in range(chunks)]
    relays, directs, sums = [], [], []
    for j, (way, other, side) in enumerate(ways):
        relays.append(scatter(0, j, block(j, far), relayed.at[j], way))
        directs.append(scatter(1, j, block(j, other), parts.at[1 - side, j], other))
        sums.append(scatter(2, j, summed.at[j], parts.at[side, j], way))
    order = [j + h * (chunks // 2) for j in range(chunks // 2) for h in range(2)]
    for j in order:
        mixed[j] = dot(gate, weight[:, j * chunk : (j + 1) * chunk]).astype(BF16)
        relays[j].start()
        directs[j].start()

    forwards = [
        pltpu.make_async_remote_copy(
            src_ref=ext.at[s, pl.ds(0, 8)],
            dst_ref=beyond.at[s],
            send_sem=beyond_sems.at[0, s],
            recv_sem=beyond_sems.at[1, s],
            device_id={"seq": lax.rem(me + n - 1, n)},
            device_id_type=MESH,
        )
        for s in range(3)
    ]
    stores = [
        pltpu.make_async_copy(source, target, store_sems.at[i])
        for i, (source, target) in enumerate((
            (results.at[0], query_out),
            (results.at[1], key_out),
            (results.at[2], value_out),
            (send.at[5, me], lags.at[me]),
            (total, mixed_out),
        ))
    ]

    def lengthen(s):
        forwards[s].wait_recv()
        ext[s, pl.ds(tokens, 8)] = jnp.where(me < n - 1, beyond[s], 0.0)
        results[s] = (
            short[s, 0:1, :] * ext[s, pl.ds(0, tokens)]
            + short[s, 1:2, :] * ext[s, pl.ds(1, tokens)]
            + short[s, 2:3, :] * ext[s, pl.ds(2, tokens)]
        ).astype(BF16)
        stores[s].start()

    ext[0, pl.ds(0, tokens)] = grad_gate[...] * response[...]
    forwards[0].start()
    everything[3].wait_recv()
    spectrum(n, recv.at[3], tabs, rowed, mid, grad_spec)
    for i, other in ((4, tap_spec), (5, sig_spec)):
        ar, ai = other[:, :width], other[:, width:]
        br, bi = grad_spec[:, :width], grad_spec[:, width:]
        mid[:, :width] = ar * br + ai * bi
        mid[:, width:] = ar * bi - ai * br
        synthesis(n, tabs, rowed, mid, send.at[i])
        exchange_start(me, n, send.at[i], landing[i], sems.at[i], keep=i < 5)
    stores[3].start()
    for j in order:
        relays[j].wait_recv()
        own_term = block(j, ways[j][0])[...].astype(F32)
        summed[j] = (own_term + relayed[j].astype(F32)).astype(BF16)
        sums[j].start()
    lengthen(0)
    grad_signal = gain[...] * (grad_gate[...] * q_short[...].astype(F32))
    everything[4].wait_recv()
    grad_signal += unpack(recv.at[4], n)
    ext[1, pl.ds(0, tokens)] = grad_signal * v_short[...].astype(F32)
    forwards[1].start()
    ext[2, pl.ds(0, tokens)] = grad_signal * k_short[...].astype(F32)
    forwards[2].start()
    lengthen(1)
    lengthen(2)
    for j in order:
        directs[j].wait_recv()
        sums[j].wait_recv()
        added = parts[0, j].astype(F32) + parts[1, j].astype(F32)
        added += block(j, part)[...].astype(F32)
        total[:, j * chunk : (j + 1) * chunk] = added.astype(BF16)
    stores[4].start()
    everything[5].wait_recv()
    for copy in gathers + passed + edges + relays + directs + sums + everything + forwards:
        copy.wait_send()
    for store in stores:
        store.wait()


def finish(n, *refs):
    sources, targets, held, taps, sems = refs[:5], refs[5:10], refs[10:15], refs[15], refs[16]
    loads = [
        pltpu.make_async_copy(source, kept, sems.at[0, i])
        for i, (source, kept) in enumerate(zip(sources, held))
    ]
    stores = [
        pltpu.make_async_copy(kept, target, sems.at[1, i])
        for i, (kept, target) in enumerate(zip(held[:4] + (taps,), targets))
    ]
    for i in (4, 0, 1, 2, 3):
        loads[i].start()
    loads[4].wait()
    taps[...] = unpack(held[4], n) * (1.0 / math.sqrt(taps.shape[0] * n))
    stores[4].start()
    for load, store in zip(loads[:4], stores):
        load.wait()
        store.start()
    for store in stores:
        store.wait()


def hbm(count):
    return [pl.BlockSpec(memory_space=pltpu.HBM)] * count


def body(query_in, key_in, value_in, short_filter, skip_gain, filter_taps, out_weight, out_grad):
    n, m = lax.axis_size("seq"), lax.axis_size("tp")
    tokens, channels = query_in.shape
    features = out_weight.shape[1]
    tabs = tables(n, tokens)
    bins = 8 * tabs[1].shape[1]
    chunks = 4
    own = tokens // m
    kept = pltpu.VMEM
    outputs = (
        [jax.ShapeDtypeStruct((own, features), BF16)]
        + [jax.ShapeDtypeStruct((tokens, channels), BF16)] * 3
        + [jax.ShapeDtypeStruct((tokens, channels), F32)]
    )
    raw = outputs[:4] + [jax.ShapeDtypeStruct((n, 16, LANES), BF16)]
    limit = pltpu.CompilerParams(
        collective_id=0, has_side_effects=True, vmem_limit_bytes=58 * 1024 * 1024
    )
    held = pl.pallas_call(
        functools.partial(operator, n, m),
        out_shape=raw,
        in_specs=hbm(13),
        out_specs=hbm(5),
        scratch_shapes=[
            kept((3, tokens + 8, channels), F32),
            kept((2, chunks, own, features // chunks), BF16),
            kept((chunks, own, features // chunks), BF16),
            kept((chunks, own, features // chunks), BF16),
            kept((own, features), BF16),
            kept((3, tokens, channels), BF16),
            kept((3, tokens, channels), BF16),
            kept((tokens, channels), F32),
            kept(short_filter.shape, F32),
            kept((1, channels), F32),
            kept(out_weight.shape, BF16),
            kept((tokens, features), BF16),
        ]
        + [kept(t.shape, t.dtype) for t in tabs]
        + [
            kept((3, 16, channels), BF16),
            kept((3, 8, channels), F32),
            kept((tokens + 8, channels), F32),
        ]
        + [kept((tokens, channels), BF16)] * 3
        + [kept((tokens, channels), F32)] * 2
        + [kept((chunks, tokens, features // chunks), BF16)]
        + [kept((bins, 2 * tokens), F32)] * 3
        + [
            kept((16 * n, LANES), F32),
            kept((bins, 2 * tokens), F32),
            kept((6, n, 16, LANES), BF16),
            kept((5, n, 16, LANES), BF16),
            pltpu.SemaphoreType.DMA((13,)),
            pltpu.SemaphoreType.DMA((2, 6)),
            pltpu.SemaphoreType.DMA((2, chunks, 3)),
            pltpu.SemaphoreType.DMA((2, 3)),
            pltpu.SemaphoreType.DMA((2, 3)),
            pltpu.SemaphoreType.DMA((6, 2)),
            pltpu.SemaphoreType.DMA((5,)),
        ],
        compiler_params=limit,
        name="operator",
    )(
        query_in, key_in, value_in, filter_taps, short_filter, skip_gain[None], out_weight,
        out_grad, *tabs,
    )
    return pl.pallas_call(
        functools.partial(finish, n),
        out_shape=outputs,
        in_specs=hbm(5),
        out_specs=hbm(5),
        scratch_shapes=[kept(o.shape, o.dtype) for o in raw + outputs[4:]]
        + [pltpu.SemaphoreType.DMA((2, 5))],
        compiler_params=pltpu.CompilerParams(vmem_limit_bytes=58 * 1024 * 1024),
        name="finish",
    )(*held)


def solution(mesh):
    in_specs = (
        P("seq", "tp"),
        P("seq", "tp"),
        P("seq", "tp"),
        P(None, None, "tp"),
        P("tp"),
        P("seq", "tp"),
        P("tp", None),
        P(("seq", "tp"), None),
    )
    out_specs = (
        P(("seq", "tp"), None),
        P("seq", "tp"),
        P("seq", "tp"),
        P("seq", "tp"),
        P("seq", "tp"),
    )
    return jax.shard_map(body, mesh=mesh, in_specs=in_specs, out_specs=out_specs, check_vma=False)
```

```python
import functools
import math

import jax
import jax.numpy as jnp
import numpy as np
from jax import lax
from jax.experimental import pallas as pl
from jax.experimental.pallas import tpu as pltpu
from jax.sharding import PartitionSpec as P

MESH = pl.DeviceIdType.MESH
BF16, F32 = jnp.bfloat16, jnp.float32
LANES = 128


def tables(shards, rows):
    outer, full = 2 * shards, 2 * shards * rows
    half = outer // 2 + 1
    padded = -(-half // 8) * 8
    freq, shard, row = np.arange(half), np.arange(shards), np.arange(rows)
    outer_angle = 2 * np.pi * (freq[:, None] * shard[None] % outer) / outer
    twist_angle = 2 * np.pi * (freq[:, None] * row[None] % full) / full
    inner_angle = 2 * np.pi * (row[:, None] * row[None] % rows) / rows
    first = np.zeros((2 * padded, shards))
    first[:half], first[padded : padded + half] = np.cos(outer_angle), -np.sin(outer_angle)
    twist = np.zeros((2, padded, rows))
    twist[0, :half], twist[1, :half] = np.cos(twist_angle), -np.sin(twist_angle)
    cos, sin = np.cos(inner_angle), -np.sin(inner_angle)
    inner = np.block([[cos, sin], [-sin, cos]])
    weight = np.full((half, 1), 2.0 / full)
    weight[0] = weight[-1] = 1.0 / full
    last = np.zeros((shards, 2 * padded))
    last[:, :half] = (weight * np.cos(outer_angle)).T
    last[:, padded : padded + half] = -(weight * np.sin(outer_angle)).T
    as_bf16 = lambda a: jnp.asarray(a.astype(np.float32)).astype(BF16)
    return (
        as_bf16(first),
        jnp.asarray(twist.astype(np.float32)),
        as_bf16(inner),
        as_bf16(inner.T),
        as_bf16(last),
    )


def dot(a, b):
    return jnp.dot(a, b, preferred_element_type=F32)


def announce(n, m):
    me, part = lax.axis_index("seq"), lax.axis_index("tp")
    barrier = pltpu.get_barrier_semaphore()
    for axis, here, count in (("tp", part, m), ("seq", me, n)):

        def greet(i, carry):
            peer = lax.rem(here + i, count)
            pl.semaphore_signal(barrier, inc=1, device_id={axis: peer}, device_id_type=MESH)
            return carry

        lax.fori_loop(1, count, greet, 0, unroll=True)
    return me, part


def exchange_start(me, n, send, recv, sems, groups=(0, 1), keep=True):
    for group in groups:
        odd = lax.rem(me + group, 2)

        def push(i, carry):
            peer = lax.rem(me + 2 * i + odd, n)
            pltpu.make_async_remote_copy(
                src_ref=send.at[peer],
                dst_ref=recv.at[me],
                send_sem=sems.at[0],
                recv_sem=sems.at[1],
                device_id={"seq": peer},
                device_id_type=MESH,
            ).start()
            return carry

        lax.fori_loop(1 - odd, n // 2, push, 0)
    if keep and 0 in groups:
        recv[pl.ds(me, 1)] = send[pl.ds(me, 1)]


def whole(me, n, send, recv, sems):
    return pltpu.make_async_remote_copy(
        src_ref=send.at[pl.ds(0, n - 1)],
        dst_ref=recv.at[pl.ds(0, n - 1)],
        send_sem=sems.at[0],
        recv_sem=sems.at[1],
        device_id={"seq": lax.rem(me + 1, n)},
        device_id_type=MESH,
    )


def pack(value, send, n):
    halves = [
        value[h * LANES : (h + 1) * LANES].T.reshape(n, 8, LANES) for h in range(2)
    ]
    send[...] = jnp.concatenate(halves, axis=1).astype(BF16)


def unpack(recv, n):
    value = recv[...].astype(F32)
    return jnp.concatenate(
        [value[:, 8 * h : 8 * h + 8].reshape(8 * n, LANES).T for h in range(2)], axis=0
    )


def spectrum(n, recv, tabs, rowed, mid, out):
    first, twist, inner = tabs[:3]
    padded = twist.shape[1]
    width = twist.shape[2]
    rowed[...] = recv[...].astype(F32).reshape(16 * n, LANES)
    for c in range(8):
        x = jnp.concatenate(
            [rowed[pl.ds(8 * h + c, n, stride=16), :] for h in range(2)], axis=1
        ).astype(BF16)
        a = dot(first[...], x)
        re, im = a[:padded], a[padded:]
        rows = pl.ds(c * padded, padded)
        mid[rows, :width] = re * twist[0] - im * twist[1]
        mid[rows, width:] = re * twist[1] + im * twist[0]
    out[...] = dot(mid[...].astype(BF16), inner[...])


def synthesis(n, tabs, rowed, mid, send):
    twist, back, last = tabs[1], tabs[3], tabs[4]
    padded = twist.shape[1]
    width = twist.shape[2]
    mid[...] = dot(mid[...].astype(BF16), back[...])
    for c in range(8):
        rows = pl.ds(c * padded, padded)
        re, im = mid[rows, :width], mid[rows, width:]
        turned = jnp.concatenate(
            [re * twist[0] + im * twist[1], im * twist[0] - re * twist[1]], axis=0
        ).astype(BF16)
        y = dot(last[...], turned)
        for h in range(2):
            rowed[pl.ds(8 * h + c, n, stride=16), :] = y[:, h * LANES : (h + 1) * LANES]
    send[...] = rowed[...].reshape(n, 16, LANES).astype(BF16)


def operator(
    n, m, query, key, value, taps_in, short_in, gain_in, weight_in, grad_in,
    first_in, twist_in, inner_in, back_in, last_in,
    mixed_out, query_out, key_out, value_out, lags,
    ext, parts, relayed, summed, total, results, streams, taps, short, gain, weight, grads, first, twist, inner, back, last,
    halo, beyond, shifted, k_short, v_short, q_short, response, grad_gate, mixed,
    tap_spec, sig_spec, grad_spec, rowed, mid, send, recv,
    load_sems, gather_sems, scatter_sems, halo_sems, beyond_sems, sems, store_sems,
):
    tabs = (first, twist, inner, back, last)
    tokens = query.shape[0]
    width = twist.shape[2]
    own = tokens // m
    chunks, chunk = mixed.shape[0], mixed.shape[2]
    me, part = lax.axis_index("seq"), lax.axis_index("tp")
    left, right, far = (lax.rem(part + d, m) for d in (3, 1, 2))
    mine = pl.ds(pl.multiple_of(part * own, own), own)
    loads = {}
    for i, (name, source, target) in enumerate((
        ("taps", taps_in, taps),
        ("key", key, streams.at[1]),
        ("value", value, streams.at[2]),
        ("short", short_in, short),
        ("gain", gain_in, gain),
        ("query", query, streams.at[0]),
        ("first", first_in, first),
        ("twist", twist_in, twist),
        ("inner", inner_in, inner),
        ("back", back_in, back),
        ("last", last_in, last),
        ("grad", grad_in, grads.at[mine]),
        ("weight", weight_in, weight),
    )):
        loads[name] = pltpu.make_async_copy(source, target, load_sems.at[i])
        loads[name].start()
        if name == "value":
            announce(n, m)
    loads["taps"].wait()
    pack(taps[...], send.at[0], n)
    pl.semaphore_wait(pltpu.get_barrier_semaphore(), n + m - 2)

    def slab(owner, h):
        start = owner * own + h * (own // 2)
        return grads.at[pl.ds(pl.multiple_of(start, own // 2), own // 2)]

    def gather(k, source, owner, h, peer):
        return pltpu.make_async_remote_copy(
            src_ref=source,
            dst_ref=slab(owner, h),
            send_sem=gather_sems.at[0, k],
            recv_sem=gather_sems.at[1, k],
            device_id={"tp": peer},
            device_id_type=MESH,
        )

    halves = [grad_in.at[pl.ds(h * (own // 2), own // 2)] for h in range(2)]
    gathers = [
        gather(0, halves[1], part, 1, right),
        gather(1, halves[0], part, 0, left),
        gather(2, halves[0], part, 0, right),
        gather(3, halves[1], part, 1, left),
    ]
    passed = [
        gather(4, slab(left, 1), left, 1, right),
        gather(5, slab(right, 0), right, 0, left),
    ]
    for copy in gathers[:2]:
        copy.start()
    edges = []
    for s, stream in enumerate((query, key, value)):
        edges.append(
            pltpu.make_async_remote_copy(
                src_ref=stream.at[pl.ds(tokens - 16, 16)],
                dst_ref=halo.at[s],
                send_sem=halo_sems.at[0, s],
                recv_sem=halo_sems.at[1, s],
                device_id={"seq": lax.rem(me + 1, n)},
                device_id_type=MESH,
            )
        )
        edges[-1].start()
    landing = [recv.at[i] for i in range(5)] + [lags]
    everything = [whole(me, n, send.at[i], landing[i], sems.at[i]) for i in range(6)]

    exchange_start(me, n, send.at[0], recv.at[0], sems.at[0], (0,))
    loads["short"].wait()
    loads["gain"].wait()

    def shorten(s, name):
        loads[name].wait()
        shifted[pl.ds(8, tokens)] = streams[s].astype(F32)
        edges[s].wait_recv()
        shifted[pl.ds(0, 8)] = jnp.where(me > 0, halo[s].astype(F32)[8:], 0.0)
        return (
            short[s, 0:1, :] * shifted[pl.ds(8, tokens)]
            + short[s, 1:2, :] * shifted[pl.ds(7, tokens)]
            + short[s, 2:3, :] * shifted[pl.ds(6, tokens)]
        ).astype(BF16)

    k_short[...] = shorten(1, "key")
    v_short[...] = shorten(2, "value")
    signal = k_short[...].astype(F32) * v_short[...].astype(F32)
    pack(signal, send.at[1], n)
    exchange_start(me, n, send.at[1], recv.at[1], sems.at[1], (0,))
    exchange_start(me, n, send.at[0], recv.at[0], sems.at[0], (1,))
    exchange_start(me, n, send.at[1], recv.at[1], sems.at[1], (1,))
    for copy in gathers[2:]:
        copy.start()
    response[...] = gain[...] * signal
    q_short[...] = shorten(0, "query")
    for name in ("first", "twist", "inner", "back", "last"):
        loads[name].wait()
    everything[0].wait_recv()
    spectrum(n, recv.at[0], tabs, rowed, mid, tap_spec)
    for arrived, copy in zip(gathers[:2], passed):
        arrived.wait_recv()
        copy.start()
    everything[1].wait_recv()
    spectrum(n, recv.at[1], tabs, rowed, mid, sig_spec)
    ar, ai = tap_spec[:, :width], tap_spec[:, width:]
    br, bi = sig_spec[:, :width], sig_spec[:, width:]
    mid[:, :width] = ar * br - ai * bi
    mid[:, width:] = ar * bi + ai * br
    synthesis(n, tabs, rowed, mid, send.at[2])
    exchange_start(me, n, send.at[2], recv.at[2], sems.at[2], (1, 0))

    loads["grad"].wait()
    loads["weight"].wait()
    for copy in gathers[2:] + passed:
        copy.wait_recv()
    grad_gate[...] = lax.dot_general(
        grads[...], weight[...], (((1,), (1,)), ((), ())), preferred_element_type=F32
    )
    pack(grad_gate[...] * q_short[...].astype(F32), send.at[3], n)
    exchange_start(me, n, send.at[3], recv.at[3], sems.at[3])

    everything[2].wait_recv()
    response[...] += unpack(recv.at[2], n)
    gate = (q_short[...].astype(F32) * response[...]).astype(BF16)

    def block(j, owner):
        return mixed.at[j, pl.ds(pl.multiple_of(owner * own, own), own)]

    def scatter(k, j, source, target, peer):
        return pltpu.make_async_remote_copy(
            src_ref=source,
            dst_ref=target,
            send_sem=scatter_sems.at[0, j, k],
            recv_sem=scatter_sems.at[1, j, k],
            device_id={"tp": peer},
            device_id_type=MESH,
        )

    ways = [(left, right, 1) if j < chunks // 2 else (right, left, 0) for j in range(chunks)]
    relays, directs, sums = [], [], []
    for j, (way, other, side) in enumerate(ways):
        relays.append(scatter(0, j, block(j, far), relayed.at[j], way))
        directs.append(scatter(1, j, block(j, other), parts.at[1 - side, j], other))
        sums.append(scatter(2, j, summed.at[j], parts.at[side, j], way))
    order = [j + h * (chunks // 2) for j in range(chunks // 2) for h in range(2)]
    for j in order:
        mixed[j] = dot(gate, weight[:, j * chunk : (j + 1) * chunk]).astype(BF16)
        relays[j].start()
        directs[j].start()

    forwards = [
        pltpu.make_async_remote_copy(
            src_ref=ext.at[s, pl.ds(0, 8)],
            dst_ref=beyond.at[s],
            send_sem=beyond_sems.at[0, s],
            recv_sem=beyond_sems.at[1, s],
            device_id={"seq": lax.rem(me + n - 1, n)},
            device_id_type=MESH,
        )
        for s in range(3)
    ]
    stores = [
        pltpu.make_async_copy(source, target, store_sems.at[i])
        for i, (source, target) in enumerate((
            (results.at[0], query_out),
            (results.at[1], key_out),
            (results.at[2], value_out),
            (send.at[5, me], lags.at[me]),
            (total, mixed_out),
        ))
    ]

    def lengthen(s):
        forwards[s].wait_recv()
        ext[s, pl.ds(tokens, 8)] = jnp.where(me < n - 1, beyond[s], 0.0)
        results[s] = (
            short[s, 0:1, :] * ext[s, pl.ds(0, tokens)]
            + short[s, 1:2, :] * ext[s, pl.ds(1, tokens)]
            + short[s, 2:3, :] * ext[s, pl.ds(2, tokens)]
        ).astype(BF16)
        stores[s].start()

    ext[0, pl.ds(0, tokens)] = grad_gate[...] * response[...]
    forwards[0].start()
    everything[3].wait_recv()
    spectrum(n, recv.at[3], tabs, rowed, mid, grad_spec)
    for i, other in ((4, tap_spec), (5, sig_spec)):
        ar, ai = other[:, :width], other[:, width:]
        br, bi = grad_spec[:, :width], grad_spec[:, width:]
        mid[:, :width] = ar * br + ai * bi
        mid[:, width:] = ar * bi - ai * br
        synthesis(n, tabs, rowed, mid, send.at[i])
        exchange_start(me, n, send.at[i], landing[i], sems.at[i], keep=i < 5)
    stores[3].start()
    for j in order:
        relays[j].wait_recv()
        own_term = block(j, ways[j][0])[...].astype(F32)
        summed[j] = (own_term + relayed[j].astype(F32)).astype(BF16)
        sums[j].start()
    lengthen(0)
    grad_signal = gain[...] * (grad_gate[...] * q_short[...].astype(F32))
    everything[4].wait_recv()
    grad_signal += unpack(recv.at[4], n)
    ext[1, pl.ds(0, tokens)] = grad_signal * v_short[...].astype(F32)
    forwards[1].start()
    ext[2, pl.ds(0, tokens)] = grad_signal * k_short[...].astype(F32)
    forwards[2].start()
    lengthen(1)
    lengthen(2)
    for j in order:
        directs[j].wait_recv()
        sums[j].wait_recv()
        added = parts[0, j].astype(F32) + parts[1, j].astype(F32)
        added += block(j, part)[...].astype(F32)
        total[:, j * chunk : (j + 1) * chunk] = added.astype(BF16)
    stores[4].start()
    everything[5].wait_recv()
    for copy in gathers + passed + edges + relays + directs + sums + everything + forwards:
        copy.wait_send()
    for store in stores:
        store.wait()


def finish(n, *refs):
    sources, targets, held, taps, sems = refs[:5], refs[5:10], refs[10:15], refs[15], refs[16]
    loads = [
        pltpu.make_async_copy(source, kept, sems.at[0, i])
        for i, (source, kept) in enumerate(zip(sources, held))
    ]
    stores = [
        pltpu.make_async_copy(kept, target, sems.at[1, i])
        for i, (kept, target) in enumerate(zip(held[:4] + (taps,), targets))
    ]
    for i in (4, 0, 1, 2, 3):
        loads[i].start()
    loads[4].wait()
    taps[...] = unpack(held[4], n) * (1.0 / math.sqrt(taps.shape[0] * n))
    stores[4].start()
    for load, store in zip(loads[:4], stores):
        load.wait()
        store.start()
    for store in stores:
        store.wait()


def hbm(count):
    return [pl.BlockSpec(memory_space=pltpu.HBM)] * count


def body(query_in, key_in, value_in, short_filter, skip_gain, filter_taps, out_weight, out_grad):
    n, m = lax.axis_size("seq"), lax.axis_size("tp")
    tokens, channels = query_in.shape
    features = out_weight.shape[1]
    tabs = tables(n, tokens)
    bins = 8 * tabs[1].shape[1]
    chunks = 4
    own = tokens // m
    kept = pltpu.VMEM
    outputs = (
        [jax.ShapeDtypeStruct((own, features), BF16)]
        + [jax.ShapeDtypeStruct((tokens, channels), BF16)] * 3
        + [jax.ShapeDtypeStruct((tokens, channels), F32)]
    )
    raw = outputs[:4] + [jax.ShapeDtypeStruct((n, 16, LANES), BF16)]
    limit = pltpu.CompilerParams(
        collective_id=0, has_side_effects=True, vmem_limit_bytes=58 * 1024 * 1024
    )
    held = pl.pallas_call(
        functools.partial(operator, n, m),
        out_shape=raw,
        in_specs=hbm(13),
        out_specs=hbm(5),
        scratch_shapes=[
            kept((3, tokens + 8, channels), F32),
            kept((2, chunks, own, features // chunks), BF16),
            kept((chunks, own, features // chunks), BF16),
            kept((chunks, own, features // chunks), BF16),
            kept((own, features), BF16),
            kept((3, tokens, channels), BF16),
            kept((3, tokens, channels), BF16),
            kept((tokens, channels), F32),
            kept(short_filter.shape, F32),
            kept((1, channels), F32),
            kept(out_weight.shape, BF16),
            kept((tokens, features), BF16),
        ]
        + [kept(t.shape, t.dtype) for t in tabs]
        + [
            kept((3, 16, channels), BF16),
            kept((3, 8, channels), F32),
            kept((tokens + 8, channels), F32),
        ]
        + [kept((tokens, channels), BF16)] * 3
        + [kept((tokens, channels), F32)] * 2
        + [kept((chunks, tokens, features // chunks), BF16)]
        + [kept((bins, 2 * tokens), F32)] * 3
        + [
            kept((16 * n, LANES), F32),
            kept((bins, 2 * tokens), F32),
            kept((6, n, 16, LANES), BF16),
            kept((5, n, 16, LANES), BF16),
            pltpu.SemaphoreType.DMA((13,)),
            pltpu.SemaphoreType.DMA((2, 6)),
            pltpu.SemaphoreType.DMA((2, chunks, 3)),
            pltpu.SemaphoreType.DMA((2, 3)),
            pltpu.SemaphoreType.DMA((2, 3)),
            pltpu.SemaphoreType.DMA((6, 2)),
            pltpu.SemaphoreType.DMA((5,)),
        ],
        compiler_params=limit,
        name="operator",
    )(
        query_in, key_in, value_in, filter_taps, short_filter, skip_gain[None], out_weight,
        out_grad, *tabs,
    )
    return pl.pallas_call(
        functools.partial(finish, n),
        out_shape=outputs,
        in_specs=hbm(5),
        out_specs=hbm(5),
        scratch_shapes=[kept(o.shape, o.dtype) for o in raw + outputs[4:]]
        + [pltpu.SemaphoreType.DMA((2, 5))],
        compiler_params=pltpu.CompilerParams(vmem_limit_bytes=58 * 1024 * 1024),
        name="finish",
    )(*held)


def solution(mesh):
    in_specs = (
        P("seq", "tp"),
        P("seq", "tp"),
        P("seq", "tp"),
        P(None, None, "tp"),
        P("tp"),
        P("seq", "tp"),
        P("tp", None),
        P(("seq", "tp"), None),
    )
    out_specs = (
        P(("seq", "tp"), None),
        P("seq", "tp"),
        P("seq", "tp"),
        P("seq", "tp"),
        P("seq", "tp"),
    )
    return jax.shard_map(body, mesh=mesh, in_specs=in_specs, out_specs=out_specs, check_vma=False)
```

```python
import functools
import math

import jax
import jax.numpy as jnp
import numpy as np
from jax import lax
from jax.experimental import pallas as pl
from jax.experimental.pallas import tpu as pltpu
from jax.sharding import PartitionSpec as P

MESH = pl.DeviceIdType.MESH
BF16, F32 = jnp.bfloat16, jnp.float32
LANES = 128


def tables(shards, rows):
    outer, full = 2 * shards, 2 * shards * rows
    half = outer // 2 + 1
    padded = -(-half // 8) * 8
    freq, shard, row = np.arange(half), np.arange(shards), np.arange(rows)
    outer_angle = 2 * np.pi * (freq[:, None] * shard[None] % outer) / outer
    twist_angle = 2 * np.pi * (freq[:, None] * row[None] % full) / full
    inner_angle = 2 * np.pi * (row[:, None] * row[None] % rows) / rows
    first = np.zeros((2 * padded, shards))
    first[:half], first[padded : padded + half] = np.cos(outer_angle), -np.sin(outer_angle)
    twist = np.zeros((2, padded, rows))
    twist[0, :half], twist[1, :half] = np.cos(twist_angle), -np.sin(twist_angle)
    cos, sin = np.cos(inner_angle), -np.sin(inner_angle)
    inner = np.block([[cos, sin], [-sin, cos]])
    weight = np.full((half, 1), 2.0 / full)
    weight[0] = weight[-1] = 1.0 / full
    last = np.zeros((shards, 2 * padded))
    last[:, :half] = (weight * np.cos(outer_angle)).T
    last[:, padded : padded + half] = -(weight * np.sin(outer_angle)).T
    as_bf16 = lambda a: jnp.asarray(a.astype(np.float32)).astype(BF16)
    return (
        as_bf16(first),
        jnp.asarray(twist.astype(np.float32)),
        as_bf16(inner),
        as_bf16(inner.T),
        as_bf16(last),
    )


def dot(a, b):
    return jnp.dot(a, b, preferred_element_type=F32)


def announce(n, m):
    me, part = lax.axis_index("seq"), lax.axis_index("tp")
    barrier = pltpu.get_barrier_semaphore()
    for axis, here, count in (("tp", part, m), ("seq", me, n)):

        def greet(i, carry):
            peer = lax.rem(here + i, count)
            pl.semaphore_signal(barrier, inc=1, device_id={axis: peer}, device_id_type=MESH)
            return carry

        lax.fori_loop(1, count, greet, 0, unroll=True)
    return me, part


def exchange_start(me, n, send, recv, sems, groups=(0, 1), keep=True):
    for group in groups:
        odd = lax.rem(me + group, 2)

        def push(i, carry):
            peer = lax.rem(me + 2 * i + odd, n)
            pltpu.make_async_remote_copy(
                src_ref=send.at[peer],
                dst_ref=recv.at[me],
                send_sem=sems.at[0],
                recv_sem=sems.at[1],
                device_id={"seq": peer},
                device_id_type=MESH,
            ).start()
            return carry

        lax.fori_loop(1 - odd, n // 2, push, 0)
    if keep and 0 in groups:
        recv[pl.ds(me, 1)] = send[pl.ds(me, 1)]


def whole(me, n, send, recv, sems):
    return pltpu.make_async_remote_copy(
        src_ref=send.at[pl.ds(0, n - 1)],
        dst_ref=recv.at[pl.ds(0, n - 1)],
        send_sem=sems.at[0],
        recv_sem=sems.at[1],
        device_id={"seq": lax.rem(me + 1, n)},
        device_id_type=MESH,
    )


def pack(value, send, n):
    halves = [
        value[h * LANES : (h + 1) * LANES].T.reshape(n, 8, LANES) for h in range(2)
    ]
    send[...] = jnp.concatenate(halves, axis=1).astype(BF16)


def unpack(recv, n):
    value = recv[...].astype(F32)
    return jnp.concatenate(
        [value[:, 8 * h : 8 * h + 8].reshape(8 * n, LANES).T for h in range(2)], axis=0
    )


def spectrum(n, recv, tabs, rowed, mid, out):
    first, twist, inner = tabs[:3]
    padded = twist.shape[1]
    width = twist.shape[2]
    rowed[pl.ds(0, 16 * n)] = recv[...].astype(F32).reshape(16 * n, LANES)
    for c in range(8):
        x = jnp.concatenate(
            [rowed[pl.ds(8 * h + c, n, stride=16), :] for h in range(2)], axis=1
        ).astype(BF16)
        a = dot(first[...], x)
        re, im = a[:padded], a[padded:]
        rows = pl.ds(c * padded, padded)
        mid[rows, :width] = re * twist[0] - im * twist[1]
        mid[rows, width:] = re * twist[1] + im * twist[0]
    out[...] = dot(mid[...].astype(BF16), inner[...])


def synthesis(n, tabs, rowed, mid, send):
    twist, back, last = tabs[1], tabs[3], tabs[4]
    padded = twist.shape[1]
    width = twist.shape[2]
    mid[...] = dot(mid[...].astype(BF16), back[...])
    for c in range(8):
        rows = pl.ds(c * padded, padded)
        re, im = mid[rows, :width], mid[rows, width:]
        turned = jnp.concatenate(
            [re * twist[0] + im * twist[1], im * twist[0] - re * twist[1]], axis=0
        ).astype(BF16)
        y = dot(last[...], turned)
        for h in range(2):
            rowed[pl.ds(8 * h + c, n, stride=16), :] = y[:, h * LANES : (h + 1) * LANES]
    send[...] = rowed[pl.ds(0, 16 * n)].reshape(n, 16, LANES).astype(BF16)


def operator(
    n, m, query, key, value, taps_in, short_in, gain_in, weight_in, grad_in,
    first_in, twist_in, inner_in, back_in, last_in,
    mixed_out, query_out, key_out, value_out, lags,
    ext, parts, relayed, summed, total, results, streams, taps, short, gain, weight, grads, first, twist, inner, back, last,
    halo, beyond, shifted, k_short, v_short, q_short, response, grad_gate, mixed,
    tap_spec, sig_spec, grad_spec, rowed, mid, send, recv,
    load_sems, gather_sems, scatter_sems, halo_sems, beyond_sems, sems, store_sems,
):
    tabs = (first, twist, inner, back, last)
    tokens = query.shape[0]
    width = twist.shape[2]
    own = tokens // m
    chunks, chunk = mixed.shape[0], mixed.shape[2]
    me, part = lax.axis_index("seq"), lax.axis_index("tp")
    left, right, far = (lax.rem(part + d, m) for d in (3, 1, 2))
    mine = pl.ds(pl.multiple_of(part * own, own), own)
    loads = {}
    for i, (name, source, target) in enumerate((
        ("taps", taps_in, taps),
        ("key", key, streams.at[1]),
        ("value", value, streams.at[2]),
        ("short", short_in, short),
        ("gain", gain_in, gain),
        ("query", query, streams.at[0]),
        ("first", first_in, first),
        ("twist", twist_in, twist),
        ("inner", inner_in, inner),
        ("back", back_in, back),
        ("last", last_in, last),
        ("grad", grad_in, grads.at[mine]),
        ("weight", weight_in, weight),
    )):
        loads[name] = pltpu.make_async_copy(source, target, load_sems.at[i])
        loads[name].start()
        if name == "value":
            announce(n, m)
    loads["taps"].wait()
    pack(taps[...], send.at[0], n)
    pl.semaphore_wait(pltpu.get_barrier_semaphore(), n + m - 2)

    def slab(owner, h):
        start = owner * own + h * (own // 2)
        return grads.at[pl.ds(pl.multiple_of(start, own // 2), own // 2)]

    def gather(k, source, owner, h, peer):
        return pltpu.make_async_remote_copy(
            src_ref=source,
            dst_ref=slab(owner, h),
            send_sem=gather_sems.at[0, k],
            recv_sem=gather_sems.at[1, k],
            device_id={"tp": peer},
            device_id_type=MESH,
        )

    halves = [grad_in.at[pl.ds(h * (own // 2), own // 2)] for h in range(2)]
    gathers = [
        gather(0, halves[1], part, 1, right),
        gather(1, halves[0], part, 0, left),
        gather(2, halves[0], part, 0, right),
        gather(3, halves[1], part, 1, left),
    ]
    passed = [
        gather(4, slab(left, 1), left, 1, right),
        gather(5, slab(right, 0), right, 0, left),
    ]
    for copy in gathers[:2]:
        copy.start()
    edges = []
    for s, stream in enumerate((query, key, value)):
        edges.append(
            pltpu.make_async_remote_copy(
                src_ref=stream.at[pl.ds(tokens - 16, 16)],
                dst_ref=halo.at[s],
                send_sem=halo_sems.at[0, s],
                recv_sem=halo_sems.at[1, s],
                device_id={"seq": lax.rem(me + 1, n)},
                device_id_type=MESH,
            )
        )
        edges[-1].start()
    landing = [recv.at[i] for i in range(5)] + [lags]
    everything = [whole(me, n, send.at[i], landing[i], sems.at[i]) for i in range(6)]

    exchange_start(me, n, send.at[0], recv.at[0], sems.at[0], (0,))
    loads["short"].wait()
    loads["gain"].wait()

    def shorten(s, name):
        loads[name].wait()
        shifted[pl.ds(8, tokens)] = streams[s].astype(F32)
        edges[s].wait_recv()
        shifted[pl.ds(0, 8)] = jnp.where(me > 0, halo[s].astype(F32)[8:], 0.0)
        return (
            short[s, 0:1, :] * shifted[pl.ds(8, tokens)]
            + short[s, 1:2, :] * shifted[pl.ds(7, tokens)]
            + short[s, 2:3, :] * shifted[pl.ds(6, tokens)]
        ).astype(BF16)

    k_short[...] = shorten(1, "key")
    v_short[...] = shorten(2, "value")
    signal = k_short[...].astype(F32) * v_short[...].astype(F32)
    pack(signal, send.at[1], n)
    exchange_start(me, n, send.at[1], recv.at[1], sems.at[1], (0,))
    exchange_start(me, n, send.at[0], recv.at[0], sems.at[0], (1,))
    exchange_start(me, n, send.at[1], recv.at[1], sems.at[1], (1,))
    for copy in gathers[2:]:
        copy.start()
    response[...] = gain[...] * signal
    q_short[...] = shorten(0, "query")
    for name in ("first", "twist", "inner", "back", "last"):
        loads[name].wait()
    everything[0].wait_recv()
    spectrum(n, recv.at[0], tabs, rowed, mid, tap_spec)
    for arrived, copy in zip(gathers[:2], passed):
        arrived.wait_recv()
        copy.start()
    everything[1].wait_recv()
    spectrum(n, recv.at[1], tabs, rowed, mid, sig_spec)
    ar, ai = tap_spec[:, :width], tap_spec[:, width:]
    br, bi = sig_spec[:, :width], sig_spec[:, width:]
    mid[:, :width] = ar * br - ai * bi
    mid[:, width:] = ar * bi + ai * br
    synthesis(n, tabs, rowed, mid, send.at[2])
    exchange_start(me, n, send.at[2], recv.at[2], sems.at[2], (1, 0))

    loads["grad"].wait()
    loads["weight"].wait()
    for copy in gathers[2:] + passed:
        copy.wait_recv()
    grad_gate[...] = lax.dot_general(
        grads[...], weight[...], (((1,), (1,)), ((), ())), preferred_element_type=F32
    )
    pack(grad_gate[...] * q_short[...].astype(F32), send.at[3], n)
    exchange_start(me, n, send.at[3], recv.at[3], sems.at[3])

    everything[2].wait_recv()
    response[...] += unpack(recv.at[2], n)
    gate = (q_short[...].astype(F32) * response[...]).astype(BF16)

    def block(j, owner):
        return mixed.at[j, pl.ds(pl.multiple_of(owner * own, own), own)]

    def scatter(k, j, source, target, peer):
        return pltpu.make_async_remote_copy(
            src_ref=source,
            dst_ref=target,
            send_sem=scatter_sems.at[0, j, k],
            recv_sem=scatter_sems.at[1, j, k],
            device_id={"tp": peer},
            device_id_type=MESH,
        )

    ways = [(left, right, 1) if j < chunks // 2 else (right, left, 0) for j in range(chunks)]
    relays, directs, sums = [], [], []
    for j, (way, other, side) in enumerate(ways):
        relays.append(scatter(0, j, block(j, far), relayed.at[j], way))
        directs.append(scatter(1, j, block(j, other), parts.at[1 - side, j], other))
        sums.append(scatter(2, j, summed.at[j], parts.at[side, j], way))
    order = [j + h * (chunks // 2) for j in range(chunks // 2) for h in range(2)]
    for j in order:
        mixed[j] = dot(gate, weight[:, j * chunk : (j + 1) * chunk]).astype(BF16)
        relays[j].start()
        directs[j].start()

    forwards = [
        pltpu.make_async_remote_copy(
            src_ref=ext.at[s, pl.ds(0, 8)],
            dst_ref=beyond.at[s],
            send_sem=beyond_sems.at[0, s],
            recv_sem=beyond_sems.at[1, s],
            device_id={"seq": lax.rem(me + n - 1, n)},
            device_id_type=MESH,
        )
        for s in range(3)
    ]
    stores = [
        pltpu.make_async_copy(source, target, store_sems.at[i])
        for i, (source, target) in enumerate((
            (results.at[0], query_out),
            (results.at[1], key_out),
            (results.at[2], value_out),
            (send.at[5, me], lags.at[me]),
            (total, mixed_out),
        ))
    ]

    def lengthen(s):
        forwards[s].wait_recv()
        ext[s, pl.ds(tokens, 8)] = jnp.where(me < n - 1, beyond[s], 0.0)
        results[s] = (
            short[s, 0:1, :] * ext[s, pl.ds(0, tokens)]
            + short[s, 1:2, :] * ext[s, pl.ds(1, tokens)]
            + short[s, 2:3, :] * ext[s, pl.ds(2, tokens)]
        ).astype(BF16)
        stores[s].start()

    ext[0, pl.ds(0, tokens)] = grad_gate[...] * response[...]
    forwards[0].start()
    everything[3].wait_recv()
    spectrum(n, recv.at[3], tabs, rowed, mid, grad_spec)
    for i, other in ((4, tap_spec), (5, sig_spec)):
        ar, ai = other[:, :width], other[:, width:]
        br, bi = grad_spec[:, :width], grad_spec[:, width:]
        mid[:, :width] = ar * br + ai * bi
        mid[:, width:] = ar * bi - ai * br
        synthesis(n, tabs, rowed, mid, send.at[i])
        exchange_start(me, n, send.at[i], landing[i], sems.at[i], keep=i < 5)
    stores[3].start()
    for j in order:
        relays[j].wait_recv()
        own_term = block(j, ways[j][0])[...].astype(F32)
        summed[j] = (own_term + relayed[j].astype(F32)).astype(BF16)
        sums[j].start()
    lengthen(0)
    grad_signal = gain[...] * (grad_gate[...] * q_short[...].astype(F32))
    everything[4].wait_recv()
    grad_signal += unpack(recv.at[4], n)
    ext[1, pl.ds(0, tokens)] = grad_signal * v_short[...].astype(F32)
    forwards[1].start()
    ext[2, pl.ds(0, tokens)] = grad_signal * k_short[...].astype(F32)
    forwards[2].start()
    lengthen(1)
    lengthen(2)
    for j in order:
        directs[j].wait_recv()
        sums[j].wait_recv()
        added = parts[0, j].astype(F32) + parts[1, j].astype(F32)
        added += block(j, part)[...].astype(F32)
        total[:, j * chunk : (j + 1) * chunk] = added.astype(BF16)
    stores[4].start()
    everything[5].wait_recv()
    for copy in gathers + passed + edges + relays + directs + sums + everything + forwards:
        copy.wait_send()
    for store in stores:
        store.wait()


def finish(n, *refs):
    sources, targets, held, taps, sems = refs[:5], refs[5:10], refs[10:15], refs[15], refs[16]
    loads = [
        pltpu.make_async_copy(source, kept, sems.at[0, i])
        for i, (source, kept) in enumerate(zip(sources, held))
    ]
    stores = [
        pltpu.make_async_copy(kept, target, sems.at[1, i])
        for i, (kept, target) in enumerate(zip(held[:4] + (taps,), targets))
    ]
    for i in (4, 0, 1, 2, 3):
        loads[i].start()
    loads[4].wait()
    taps[...] = unpack(held[4], n) * (1.0 / math.sqrt(taps.shape[0] * n))
    stores[4].start()
    for load, store in zip(loads[:4], stores):
        load.wait()
        store.start()
    for store in stores:
        store.wait()


def hbm(count):
    return [pl.BlockSpec(memory_space=pltpu.HBM)] * count


def body(query_in, key_in, value_in, short_filter, skip_gain, filter_taps, out_weight, out_grad):
    n, m = lax.axis_size("seq"), lax.axis_size("tp")
    tokens, channels = query_in.shape
    features = out_weight.shape[1]
    tabs = tables(n, tokens)
    bins = 8 * tabs[1].shape[1]
    chunks = 4
    own = tokens // m
    kept = pltpu.VMEM
    outputs = (
        [jax.ShapeDtypeStruct((own, features), BF16)]
        + [jax.ShapeDtypeStruct((tokens, channels), BF16)] * 3
        + [jax.ShapeDtypeStruct((tokens, channels), F32)]
    )
    raw = outputs[:4] + [jax.ShapeDtypeStruct((n, 16, LANES), BF16)]
    limit = pltpu.CompilerParams(
        collective_id=0, has_side_effects=True, vmem_limit_bytes=58 * 1024 * 1024
    )
    held = pl.pallas_call(
        functools.partial(operator, n, m),
        out_shape=raw,
        in_specs=hbm(13),
        out_specs=hbm(5),
        scratch_shapes=[
            kept((3, tokens + 8, channels), F32),
            kept((2, chunks, own, features // chunks), BF16),
            kept((chunks, own, features // chunks), BF16),
            kept((chunks, own, features // chunks), BF16),
            kept((own, features), BF16),
            kept((3, tokens, channels), BF16),
            kept((3, tokens, channels), BF16),
            kept((tokens, channels), F32),
            kept(short_filter.shape, F32),
            kept((1, channels), F32),
            kept(out_weight.shape, BF16),
            kept((tokens, features), BF16),
        ]
        + [kept(t.shape, t.dtype) for t in tabs]
        + [
            kept((3, 16, channels), BF16),
            kept((3, 8, channels), F32),
            kept((tokens + 8, channels), F32),
        ]
        + [kept((tokens, channels), BF16)] * 3
        + [kept((tokens, channels), F32)] * 2
        + [kept((chunks, tokens, features // chunks), BF16)]
        + [kept((bins, 2 * tokens), F32)] * 3
        + [
            kept((16 * n + 16, LANES), F32),
            kept((bins, 2 * tokens), F32),
            kept((6, n, 16, LANES), BF16),
            kept((5, n, 16, LANES), BF16),
            pltpu.SemaphoreType.DMA((13,)),
            pltpu.SemaphoreType.DMA((2, 6)),
            pltpu.SemaphoreType.DMA((2, chunks, 3)),
            pltpu.SemaphoreType.DMA((2, 3)),
            pltpu.SemaphoreType.DMA((2, 3)),
            pltpu.SemaphoreType.DMA((6, 2)),
            pltpu.SemaphoreType.DMA((5,)),
        ],
        compiler_params=limit,
        name="operator",
    )(
        query_in, key_in, value_in, filter_taps, short_filter, skip_gain[None], out_weight,
        out_grad, *tabs,
    )
    return pl.pallas_call(
        functools.partial(finish, n),
        out_shape=outputs,
        in_specs=hbm(5),
        out_specs=hbm(5),
        scratch_shapes=[kept(o.shape, o.dtype) for o in raw + outputs[4:]]
        + [pltpu.SemaphoreType.DMA((2, 5))],
        compiler_params=pltpu.CompilerParams(vmem_limit_bytes=58 * 1024 * 1024),
        name="finish",
    )(*held)


def solution(mesh):
    in_specs = (
        P("seq", "tp"),
        P("seq", "tp"),
        P("seq", "tp"),
        P(None, None, "tp"),
        P("tp"),
        P("seq", "tp"),
        P("tp", None),
        P(("seq", "tp"), None),
    )
    out_specs = (
        P(("seq", "tp"), None),
        P("seq", "tp"),
        P("seq", "tp"),
        P("seq", "tp"),
        P("seq", "tp"),
    )
    return jax.shard_map(body, mesh=mesh, in_specs=in_specs, out_specs=out_specs, check_vma=False)
```
